256 devices in a mesh: dp: 16 (over z, core), expert: 16 (over y, x).
Axes of the slice: x: 4, y: 4, z: 8, core: 2. Of those that a mesh axis runs over, the one named last changes fastest.
Arguments:
- tokens: bfloat16 [32768, 4096], P(('dp', 'expert')), may hold values from -6 to 6
- expert_ids: int32 [32768, 1], P(('dp', 'expert')), may hold values from 0 to 7; in each aligned block of 128 rows (0 to 127, 128 to 255, ...) at most 24 rows name the same one
- gate_values: float32 [32768, 1], P(('dp', 'expert')), may hold values from 0.1 to 1
- cotangent: bfloat16 [32768, 4096], P(('dp', 'expert')), may hold values from -6 to 6
- gate_weight: bfloat16 [4096, 6144], P('dp', 'expert'), may hold values from -0.09375 to 0.09375
- up_weight: bfloat16 [4096, 6144], P('dp', 'expert'), may hold values from -0.09375 to 0.09375
- down_weight: bfloat16 [4096, 6144], P('dp', 'expert'), may hold values from -0.21875 to 0.21875
Outputs:
- moe_out: bfloat16 [32768, 4096], P(('dp', 'expert'))
- token_grad: bfloat16 [32768, 4096], P(('dp', 'expert'))
- gate_grad: float32 [4096, 6144], P('dp', 'expert')
- up_grad: float32 [4096, 6144], P('dp', 'expert')
- down_grad: float32 [4096, 6144], P('dp', 'expert')
The draws below stay inside these ranges and needn't reach their ends.
Inputs may be any that keep to these rules, and one draw needn't show every extreme that they name: `expert_ids`: within each device's 128 rows no expert is named more than 24 times, and in some of those blocks one expert is named exactly 24 times.
All inputs are finite; a program needn't handle non-finite values.
Results may differ from the reference program's by a relative error of at most 0.02.
Values may be sent and summed in bfloat16 or wider, within the bound.
A program may use at most 128 MiB of HBM per device.

```python
import math
import jax
import jax.numpy as jnp
import numpy as np
from jax import lax

D = 4096
FF = 768
TOPK = 1
TOK_DEV = 128
EXPERTS = 8
CAP = 24
TOKENS = 32768
N_DP = 16
N_EXPERT = 16


def levels(own_key, shape, shards, low, high):
    gain = 1.0
    for position, shards_of in shards:
        draws = jax.random.uniform(jax.random.fold_in(jax.random.fold_in(own_key, 6), position), (shards_of,), jnp.float32, low / len(shards), high / len(shards))
        gain = gain * jnp.repeat(jnp.exp(draws), shape[position] // shards_of).reshape((-1,) + (1,) * (len(shape) - 1 - position))
    return gain


def shared_out(rng, own, number, rows, number_of, top, most, skew):
    order = jax.random.permutation(rng, number_of)
    packed, common = shares(number_of, rows * top, most, skew, True), shares(number_of, rows * top, most, skew, False)
    places = jnp.arange(number_of)

    def named(tallies, rotation):
        used = int((tallies > 0).sum())
        fixed = max(1, used // 4)
        passed = fixed + (places - fixed + rotation * (used - fixed)) % max(1, number_of - fixed)
        return jnp.zeros((number_of,), jnp.int32).at[order[jnp.where(places < fixed, places, passed)]].set(jnp.asarray(tallies, jnp.int32))

    tallies = jnp.where(number % 4 == 0, named(packed, number // 4), named(common, number - number // 4 - 1))
    mixed = jax.random.permutation(jax.random.fold_in(own, 3), number_of)
    donor, sink = mixed[0:number_of // 2 * 2:2], mixed[1:number_of // 2 * 2:2]
    room = jnp.minimum(tallies[donor] - 1, most - tallies[sink]) // 2
    room = jnp.where((donor == order[0]) | (sink == order[0]) | (tallies[sink] == 0), 0, jnp.maximum(room, 0))
    passed = jax.random.randint(jax.random.fold_in(own, 4), (number_of // 2,), 0, 1 << 20) % (room + 1)
    tallies = tallies.at[donor].add(-passed).at[sink].add(passed)
    members = jnp.searchsorted(jnp.cumsum(tallies), jnp.arange(rows * top), side="right").astype(jnp.int32)
    table = members.reshape(top, rows).T
    table = table[jax.random.permutation(jax.random.fold_in(own, 1), rows)]
    rotation = jax.random.randint(jax.random.fold_in(own, 2), (rows, 1), 0, top)
    return jnp.take_along_axis(table, (jnp.arange(top)[None, :] + rotation) % top, axis=1)


def shares(count, total, most, slope, full):
    loads = [(1 << 20) // math.isqrt(grade ** slope) + 1 for grade in range(1, count + 1)]
    largest = most if full else min(most, max(-(-total // count), total * loads[0] // sum(loads)))
    least = 1 if total - largest >= count - 1 else 0
    counts, rest = [largest] + [least] * (count - 1), total - largest - least * (count - 1)
    while rest > 0:
        candidates = [i for i in range(1, count) if counts[i] < largest] or [i for i in range(1, count) if counts[i] < most]
        pool, budget = sum([loads[i] for i in candidates]), rest
        for i in candidates:
            extra = min(most - counts[i], max(1, budget * loads[i] // pool), rest)
            counts[i] = counts[i] + extra
            rest = rest - extra
    return np.array(counts)


def scatter_about(rng, extent, spread, limit, pieces=(), held_as=jnp.bfloat16):
    drawn = spread * jax.random.normal(rng, extent, jnp.float32)
    if pieces:
        drawn = drawn * levels(rng, extent, pieces, -0.22, 0.18)
    return jnp.clip(drawn, -limit, limit).astype(held_as)


def setup_inputs(seed: int = 0) -> dict:
    key_list = jax.random.split(jax.random.key(seed), 8)
    tokens = scatter_about(key_list[0], (TOKENS, D), 1.0, 6.0, ((0, 256),))
    expert_ids_keys = jax.random.split(jax.random.fold_in(key_list[1], 1), TOKENS // TOK_DEV)
    expert_ids_turns = jax.random.permutation(jax.random.fold_in(key_list[1], 3), TOKENS // TOK_DEV)
    expert_ids = jax.vmap(lambda own, number: shared_out(jax.random.fold_in(key_list[1], 2), own, number, TOK_DEV, EXPERTS, TOPK, CAP, 2))(expert_ids_keys, expert_ids_turns).reshape((TOKENS, TOPK))
    gate_values = jnp.clip(jnp.exp(math.log(1.0) - 2.3025851 * jax.random.uniform(key_list[2], (TOKENS, TOPK), jnp.float32) ** levels(key_list[2], (TOKENS, TOPK), ((0, 256),), -0.2, 0.2)), 0.1, 1.0)
    cotangent = scatter_about(key_list[3], (TOKENS, D), 1.0, 6.0, ((0, 256),))
    gate_weight = scatter_about(key_list[4], (D, EXPERTS * FF), D ** -0.5, 0.09375, ((0, 16), (1, 16)))
    up_weight = scatter_about(key_list[5], (D, EXPERTS * FF), D ** -0.5, 0.09375, ((0, 16), (1, 16)))
    down_weight = scatter_about(key_list[6], (D, EXPERTS * FF), FF ** -0.5, 0.21875, ((0, 16), (1, 16)))
    return dict(tokens=tokens, expert_ids=expert_ids, gate_values=gate_values, cotangent=cotangent, gate_weight=gate_weight, up_weight=up_weight, down_weight=down_weight)


def reference(tokens, expert_ids, gate_values, cotangent, gate_weight, up_weight, down_weight):
    group = TOK_DEV * N_EXPERT
    rows_all = N_EXPERT * CAP
    half_units = FF // 2
    highest = lax.Precision.HIGHEST
    gate_full = gate_weight.astype(jnp.float32).reshape(D, EXPERTS, FF)
    up_full = up_weight.astype(jnp.float32).reshape(D, EXPERTS, FF)
    down_full = down_weight.astype(jnp.float32).reshape(D, EXPERTS, FF)

    def per_group(carry, inputs):
        tok_group, ids_group, val_group, cot_group = inputs
        flat_ids = ids_group.reshape(N_EXPERT, TOK_DEV * TOPK)
        onehot = (flat_ids[:, :, None] == jnp.arange(EXPERTS, dtype=jnp.int32)[None, None, :]).astype(jnp.int32)
        before = jnp.cumsum(onehot, axis=1) - onehot
        order = jnp.sum(before * onehot, axis=2)
        block_base = jnp.arange(N_EXPERT, dtype=jnp.int32)[:, None] * CAP
        slot_index = (flat_ids * rows_all + block_base + order).reshape(-1).astype(jnp.int32)
        source_rows = jnp.broadcast_to(tok_group[:, None, :], (group, TOPK, D)).reshape(group * TOPK, D)
        expert_in = jnp.zeros((EXPERTS * rows_all, D), jnp.bfloat16).at[slot_index].set(source_rows)
        inputs_f = expert_in.reshape(EXPERTS, rows_all, D).astype(jnp.float32)
        gate_pre = jnp.einsum('erd,def->erf', inputs_f, gate_full, precision=highest)
        up_pre = jnp.einsum('erd,def->erf', inputs_f, up_full, precision=highest)
        sigmoid_g = jax.nn.sigmoid(gate_pre)
        silu_g = gate_pre * sigmoid_g
        hidden = (silu_g * up_pre).astype(jnp.bfloat16)
        hidden_f = hidden.astype(jnp.float32)
        first = jnp.einsum('erf,def->erd', hidden_f[:, :, :half_units], down_full[:, :, :half_units], precision=highest).astype(jnp.bfloat16)
        second = jnp.einsum('erf,def->erd', hidden_f[:, :, half_units:], down_full[:, :, half_units:], precision=highest).astype(jnp.bfloat16)
        expert_out = (first.astype(jnp.float32) + second.astype(jnp.float32)).astype(jnp.bfloat16)
        out_flat = expert_out.reshape(EXPERTS * rows_all, D).astype(jnp.float32)
        picked = out_flat[slot_index].reshape(group, TOPK, D)
        moe_group = jnp.sum(val_group[:, :, None] * picked, axis=1).astype(jnp.bfloat16)
        grad_source = (val_group[:, :, None] * cot_group.astype(jnp.float32)[:, None, :]).astype(jnp.bfloat16)
        grad_out = jnp.zeros((EXPERTS * rows_all, D), jnp.bfloat16).at[slot_index].set(grad_source.reshape(group * TOPK, D))
        grad_out_f = grad_out.reshape(EXPERTS, rows_all, D).astype(jnp.float32)
        grad_hidden = jnp.einsum('erd,def->erf', grad_out_f, down_full, precision=highest)
        grad_gate = (grad_hidden * up_pre * sigmoid_g * (1.0 + gate_pre * (1.0 - sigmoid_g))).astype(jnp.bfloat16)
        grad_up = (grad_hidden * silu_g).astype(jnp.bfloat16)
        grad_gate_f = grad_gate.astype(jnp.float32)
        grad_up_f = grad_up.astype(jnp.float32)

        def back_half(lower, upper):
            part_gate = jnp.einsum('erf,def->erd', grad_gate_f[:, :, lower:upper], gate_full[:, :, lower:upper], precision=highest)
            part_up = jnp.einsum('erf,def->erd', grad_up_f[:, :, lower:upper], up_full[:, :, lower:upper], precision=highest)
            return (part_gate + part_up).astype(jnp.bfloat16)

        grad_first = back_half(0, half_units)
        grad_second = back_half(half_units, FF)
        grad_in = (grad_first.astype(jnp.float32) + grad_second.astype(jnp.float32)).astype(jnp.bfloat16)
        grad_flat = grad_in.reshape(EXPERTS * rows_all, D).astype(jnp.float32)
        token_group = jnp.sum(grad_flat[slot_index].reshape(group, TOPK, D), axis=1).astype(jnp.bfloat16)

        def term(left, right):
            value = jnp.einsum('erd,erf->def', left, right, precision=highest).astype(jnp.bfloat16)
            value = lax.optimization_barrier(value)
            return value.astype(jnp.float32).reshape(D, EXPERTS * FF)

        gate_acc, up_acc, down_acc = carry
        gate_acc = gate_acc + term(inputs_f, grad_gate_f)
        up_acc = up_acc + term(inputs_f, grad_up_f)
        down_acc = down_acc + term(grad_out_f, hidden_f)
        return (gate_acc, up_acc, down_acc), (moe_group, token_group)

    zeros_acc = jnp.zeros((D, EXPERTS * FF), jnp.float32)
    inputs = (tokens.reshape(N_DP, group, D), expert_ids.reshape(N_DP, group, TOPK).astype(jnp.int32),
              gate_values.reshape(N_DP, group, TOPK), cotangent.reshape(N_DP, group, D))
    sums, outputs = lax.scan(per_group, (zeros_acc, zeros_acc, zeros_acc), inputs)
    moe_out = outputs[0].reshape(TOKENS, D)
    token_grad = outputs[1].reshape(TOKENS, D)
    return (moe_out, token_grad, sums[0], sums[1], sums[2])
```

```python
import functools

import jax
import jax.numpy as jnp
from jax import lax
from jax.experimental import pallas as pl
from jax.experimental.pallas import tpu as pltpu
from jax.sharding import PartitionSpec as P

MESH = pl.DeviceIdType.MESH
BF, F32 = jnp.bfloat16, jnp.float32
HOPS = ({1: 4, -1: 3}, {1: 3, -1: 4}, {1: 4, -1: 3})
TOK, OUT = 0, 0
COT, GRAD = 1, 1
OWN, PAR, NBR, FWD = 0, 1, 2, 3
CAP = 24
SLAB = 2 * CAP
BLK = 256
N_SEM = 190


def kernel(
    tok, ids, gv, cot, wg, wu, wd,
    o_moe, o_tok, o_gate, o_up, o_down,
    w_all, s_buf, own_buf, oth_buf, par_buf, nbr_buf, fwd_buf, x_buf, part, back_own, back_nbr,
    back_oth, res, sib_buf, ring_buf, pre, act, sel, ssem, rsem, lsem,
):
    nz = w_all.shape[1]
    units = wg.shape[1]
    half = s_buf.shape[-1]
    rows = x_buf.shape[1]
    tiles = half // BLK
    dp, ex = lax.axis_index("dp"), lax.axis_index("expert")
    z, c = lax.div(dp, 2), lax.rem(dp, 2)
    y, x = lax.div(ex, 4), lax.rem(ex, 4)
    p = lax.div(x, 2)
    partner = (dp, ex + 1 - 2 * lax.rem(x, 2))
    neighbour = (dp, y * 4 + 3 - x)
    sibling = (dp + 1 - 2 * c, ex)

    def zdev(d):
        return (lax.rem(z + nz + d, nz) * 2 + c, ex)

    def ydev(r):
        return (dp, lax.rem(y + r, 4) * 4 + x)

    def expert_at(r, other):
        mine = lax.rem(y + r, 4) * 2 + p
        return mine + (1 - 2 * p) if other else mine

    barrier = pltpu.get_barrier_semaphore()
    for dev in (partner, neighbour, sibling, zdev(1), zdev(-1), ydev(1), ydev(2), ydev(3)):
        pl.semaphore_signal(barrier, inc=1, device_id=dev, device_id_type=MESH)
    pl.semaphore_wait(barrier, 8)

    copies, received, sent = {}, set(), set()

    def send(key, src, dst, dev):
        i = len(copies)
        copy = pltpu.make_async_remote_copy(
            src_ref=src, dst_ref=dst, send_sem=ssem.at[i], recv_sem=rsem.at[i],
            device_id=dev, device_id_type=MESH,
        )
        copy.start()
        copies[key] = copy

    def got(*key):
        if key not in received:
            received.add(key)
            copies[key].wait_recv()

    def drain(*kinds):
        for key, copy in copies.items():
            if key not in sent and (not kinds or key[0] in kinds):
                sent.add(key)
                copy.wait_send()

    shards = (wg, wu, wd)

    def cols(m):
        return slice(m * units, (m + 1) * units)

    def zpos(off):
        return lax.rem(z + nz + off, nz)

    def w_start(m):
        for d in (1, -1):
            send(("w", m, d, 1), shards[m], w_all.at[c, z, :, cols(m)], zdev(d))

    def w_arrive(m, s):
        for d in (1, -1):
            if s <= HOPS[m][d]:
                got("w", m, d, s)
                block = w_all.at[c, zpos(-d * s), :, cols(m)]
                if s < HOPS[m][d]:
                    send(("w", m, d, s + 1), block, block, zdev(d))
                send(("ws", m, d, s), block, block, sibling)

    def w_ready(m):
        for d in (1, -1):
            for s in range(1, HOPS[m][d] + 1):
                got("w", m, d, s)
                got("ws", m, d, s)
        got("ws", m, 0, 0)

    w_start(0)
    w_start(1)
    local = []
    for m in range(3):
        send(("ws", m, 0, 0), shards[m], w_all.at[c, z, :, cols(m)], sibling)
        local.append(pltpu.make_async_copy(shards[m], w_all.at[c, z, :, cols(m)], lsem.at[m]))
        local[-1].start()

    ntok = ids.shape[0]
    idv = ids[...]
    lane = lax.broadcasted_iota(jnp.int32, (ntok, 128), 1)
    onehot = jnp.where(idv == lane, 1.0, 0.0).astype(F32)
    lower = jnp.where(
        lax.broadcasted_iota(jnp.int32, (ntok, ntok), 0)
        > lax.broadcasted_iota(jnp.int32, (ntok, ntok), 1), 1.0, 0.0,
    ).astype(BF)
    before = jnp.dot(lower, onehot.astype(BF), preferred_element_type=F32)
    order = jnp.sum(before * onehot, axis=1, keepdims=True).astype(jnp.int32)
    place = idv * SLAB + order
    slot = lax.broadcasted_iota(jnp.int32, (ntok, sel.shape[2]), 1)
    for h in range(2):
        sel[h] = jnp.where(slot == place + h * CAP, 1.0, 0.0).astype(BF)

    def dispatch(ph, source):
        def body(j, carry):
            acc = None
            for h in range(2):
                at = pl.ds(pl.multiple_of(h * half + j * BLK, BLK), BLK)
                term = lax.dot_general(
                    sel[h], source(at), (((0,), (0,)), ((), ())), preferred_element_type=F32
                )
                acc = term if acc is None else acc + term
            at = pl.ds(pl.multiple_of(j * BLK, BLK), BLK)
            s_buf[ph, :, :, at] = acc.astype(BF).reshape(8, SLAB, BLK)
            return carry

        lax.fori_loop(0, tiles, body, 0)

    def y_sends(ph):
        for r in (1, 3):
            send(("own", ph, r), s_buf.at[ph, expert_at(r, False)], own_buf.at[ph, r - 1], ydev(r))
        for r in (1, 3):
            send(("oth", ph, r), s_buf.at[ph, expert_at(r, True)], oth_buf.at[ph, r - 1], ydev(r))
        send(("own", ph, 2), s_buf.at[ph, expert_at(2, False)], own_buf.at[ph, 1], ydev(2))
        send(("oth", ph, 2), s_buf.at[ph, expert_at(2, True)], oth_buf.at[ph, 1], ydev(2))

    def self_par(ph):
        send(("par", ph, 0), s_buf.at[ph, expert_at(0, False)], par_buf.at[ph, 0], partner)

    def self_nbr(ph):
        send(("nbr", ph, 0), s_buf.at[ph, expert_at(0, True)], nbr_buf.at[ph, 0], neighbour)

    def t_own(ph, r):
        got("own", ph, r)
        send(("par", ph, r), own_buf.at[ph, r - 1], par_buf.at[ph, r], partner)

    def t_oth(ph, r):
        got("oth", ph, r)
        send(("nbr", ph, r), oth_buf.at[ph, r - 1], nbr_buf.at[ph, r], neighbour)

    def t_nbr(ph, r):
        got("nbr", ph, r)
        send(("fwd", ph, r), nbr_buf.at[ph, r], fwd_buf.at[ph, r], partner)

    wide = 512

    def gather_rows(ph):
        for r in range(4):
            got("par", ph, r)
            got("fwd", ph, r)

        def slab(g, r, at):
            if g == OWN:
                if r == 0:
                    return s_buf[ph, expert_at(0, False), :, at]
                return own_buf[ph, r - 1, :, at]
            return {PAR: par_buf, NBR: nbr_buf, FWD: fwd_buf}[g][ph, r, :, at]

        def body(j, carry):
            at = pl.ds(pl.multiple_of(j * wide, wide), wide)
            for g in range(4):
                for r in (0, 2):
                    first = slab(g, r, at).astype(F32)
                    second = slab(g, r + 1, at).astype(F32)
                    base = (g * 4 + r) * CAP
                    for h in range(2):
                        both = jnp.concatenate(
                            [first[h * CAP:(h + 1) * CAP], second[h * CAP:(h + 1) * CAP]], axis=0
                        )
                        to = pl.ds(pl.multiple_of(h * half + j * wide, wide), wide)
                        x_buf[ph, base:base + SLAB, to] = both.astype(BF)
            return carry

        lax.fori_loop(0, half // wide, body, 0)

    def project(ph, m, width):
        pre_at = slice(0, width)

        def body(j, carry):
            acc = None
            for k in range(2):
                at = pl.ds(pl.multiple_of(j * 2 * BLK + k * BLK, BLK), BLK)
                term = jnp.dot(
                    x_buf[ph, :, at], w_all[k, j, :, m * units:m * units + width],
                    preferred_element_type=F32,
                )
                acc = term if acc is None else acc + term
            pre_to[:, pre_at] += acc
            return carry

        pre_to = pre if ph == TOK else grad_hidden
        pre_to[:, pre_at] = jnp.zeros((rows, width), F32)
        lax.fori_loop(0, nz, body, 0)

    grad_hidden = pre.at[:, 2 * units:3 * units]
    tall = 32

    def activate():
        def body(i, carry):
            at = pl.ds(pl.multiple_of(i * tall, tall), tall)
            gate, up = pre[at, cols(0)], pre[at, cols(1)]
            act[at, cols(2)] = (gate * jax.nn.sigmoid(gate) * up).astype(BF)
            return carry

        lax.fori_loop(0, rows // tall, body, 0)

    def differentiate():
        def body(i, carry):
            at = pl.ds(pl.multiple_of(i * tall, tall), tall)
            gate, up, grad = pre[at, cols(0)], pre[at, cols(1)], pre[at, cols(2)]
            sig = jax.nn.sigmoid(gate)
            act[at, cols(0)] = (grad * up * sig * (1.0 + gate * (1.0 - sig))).astype(BF)
            act[at, cols(1)] = (grad * (gate * sig)).astype(BF)
            return carry

        lax.fori_loop(0, rows // tall, body, 0)

    def partials(ph, at_units):
        def body(j, carry):
            k, zz = lax.rem(j, 2), lax.div(j, 2)
            both = []
            for h in range(2):
                value = lax.dot_general(
                    act[:, at_units], w_all[k, zz + h * (nz // 2), :, at_units],
                    (((1,), (1,)), ((), ())), preferred_element_type=F32,
                )
                both.append(value.reshape(rows // CAP, CAP, BLK))
            joined = jnp.concatenate(both, axis=1).astype(BF).reshape(4, 4, SLAB, BLK)
            part[ph, :, :, :, pl.ds(pl.multiple_of(j * BLK, BLK), BLK)] = joined
            return carry

        lax.fori_loop(0, tiles, body, 0)

    def pair_sends(ph):
        for r in range(4):
            send(("bn", ph, r), part.at[ph, FWD, r], back_nbr.at[ph, r], partner)
        for r in range(4):
            send(("bo", ph, r), part.at[ph, PAR, r], back_own.at[ph, r], partner)

    def add_into(dst, a, b):
        def body(j, carry):
            at = pl.ds(pl.multiple_of(j * wide, wide), wide)
            dst[:, at] = (a[:, at].astype(F32) + b[:, at].astype(F32)).astype(BF)
            return carry

        lax.fori_loop(0, half // wide, body, 0)

    def back_n(ph, r):
        got("bn", ph, r)
        mine = part.at[ph, NBR, r]
        add_into(mine, mine, back_nbr.at[ph, r])
        send(("bx", ph, r), mine, back_oth.at[ph, r], neighbour)

    def back_o(ph, r):
        got("bo", ph, r)
        mine = part.at[ph, OWN, r]
        e = expert_at(0, False)
        if r == 0:
            add_into(res.at[ph, e], mine, back_own.at[ph, r])
        else:
            add_into(mine, mine, back_own.at[ph, r])
            send(("ro", ph, r), mine, res.at[ph, e], ydev(4 - r))

    def back_x(ph, r):
        got("bx", ph, r)
        e = expert_at(0, True)
        if r == 0:
            res[ph, e] = back_oth[ph, 0]
        else:
            send(("rx", ph, r), back_oth.at[ph, r], res.at[ph, e], ydev(4 - r))

    def combine(ph, out, scale):
        for r in (1, 2, 3):
            got("ro", ph, r)
            got("rx", ph, r)

        def body(j, carry):
            at = pl.ds(pl.multiple_of(j * BLK, BLK), BLK)
            rows_back = res[ph, :, :, at].reshape(8 * SLAB, BLK)
            for h in range(2):
                value = jnp.dot(sel[h], rows_back, preferred_element_type=F32)
                if scale:
                    value = value * gv[...]
                out[:, pl.ds(pl.multiple_of(h * half + j * BLK, BLK), BLK)] = value.astype(BF)
            return carry

        lax.fori_loop(0, tiles, body, 0)

    def offset(j):
        odd = lax.rem(j, 2)
        return 4 + lax.div(j, 2) * (1 - odd) - lax.div(j + 1, 2) * odd

    def weight_block(k, zz):
        at = pl.ds(pl.multiple_of((zz * 2 + k) * BLK, BLK), BLK)
        by_rows = (((0,), (0,)), ((), ()))
        w_all[k, zz, :, 0:2 * units] = lax.dot_general(
            x_buf[TOK, :, at], act[:, 0:2 * units], by_rows, preferred_element_type=F32
        ).astype(BF)
        w_all[k, zz, :, cols(2)] = lax.dot_general(
            x_buf[COT, :, at], act[:, cols(2)], by_rows, preferred_element_type=F32
        ).astype(BF)

    def weight_grads(k, to_sibling):
        base = len(copies)

        def piece(j, off):
            return pltpu.make_async_remote_copy(
                src_ref=w_all.at[k, zpos(off)], dst_ref=sib_buf.at[off], send_sem=ssem.at[base + j],
                recv_sem=rsem.at[base + j], device_id=sibling, device_id_type=MESH,
            )

        def body(j, carry):
            off = offset(j)
            weight_block(k, zpos(off))
            if to_sibling:
                piece(j, off).start()
            return carry

        lax.fori_loop(0, nz, body, 0)
        if to_sibling:
            for j, off in enumerate((4, 3, 5, 2, 6, 1, 7, 0)):
                copies["sib", off] = piece(j, off)

    ring_slots = {}

    def slot_of(*key):
        return ring_buf.at[ring_slots.setdefault(key, len(ring_slots))]

    def ring_send(m, s):
        for d in (1, -1):
            hops = HOPS[m][d]
            if s < hops:
                off = (d * (hops - s)) % nz
                got("sib", off)
                block = w_all.at[c, zpos(off), :, cols(m)]
                total = block[...].astype(F32) + sib_buf[off, :, cols(m)].astype(F32)
                if s > 0:
                    got("ring", m, d, s - 1)
                    total = total + slot_of(m, d, s - 1)[...].astype(F32)
                block[...] = total.astype(BF)
                send(("ring", m, d, s), block, slot_of(m, d, s), zdev(d))

    def ring_end(m, out):
        got("sib", 0)
        total = w_all[c, z, :, cols(m)].astype(F32) + sib_buf[0, :, cols(m)].astype(F32)
        for d in (1, -1):
            last = HOPS[m][d] - 1
            got("ring", m, d, last)
            total = total + slot_of(m, d, last)[...].astype(F32)
        out[...] = total

    dispatch(TOK, lambda at: tok[:, at])
    self_par(TOK)
    self_nbr(TOK)
    y_sends(TOK)
    dispatch(COT, lambda at: (gv[...] * cot[:, at].astype(F32)).astype(BF))
    w_arrive(0, 1)
    t_own(TOK, 1)
    t_own(TOK, 3)
    t_nbr(TOK, 0)
    w_arrive(1, 1)
    t_oth(TOK, 1)
    t_oth(TOK, 3)
    w_arrive(0, 2)
    t_own(TOK, 2)
    t_nbr(TOK, 1)
    t_oth(TOK, 2)
    w_arrive(1, 2)
    t_nbr(TOK, 3)
    y_sends(COT)
    self_nbr(COT)
    w_arrive(0, 3)
    t_nbr(TOK, 2)
    w_arrive(1, 3)
    self_par(COT)
    w_start(2)
    t_own(COT, 1)
    t_own(COT, 3)
    t_oth(COT, 1)
    t_oth(COT, 3)
    w_arrive(0, 4)
    w_arrive(1, 4)
    t_own(COT, 2)
    t_oth(COT, 2)
    t_nbr(COT, 0)
    gather_rows(TOK)
    w_arrive(2, 1)
    t_nbr(COT, 1)
    for copy in local:
        copy.wait()
    w_ready(0)
    w_ready(1)
    project(TOK, 0, 2 * units)
    w_arrive(2, 2)
    t_nbr(COT, 3)
    t_nbr(COT, 2)
    activate()
    w_arrive(2, 3)
    w_arrive(2, 4)
    w_ready(2)
    partials(OUT, cols(2))
    gather_rows(COT)
    pair_sends(OUT)
    project(COT, 2, units)
    differentiate()
    partials(GRAD, slice(0, 2 * units))
    pair_sends(GRAD)
    drain("w", "ws")
    weight_grads(1 - c, True)
    weight_grads(c, False)
    for m in range(3):
        ring_send(m, 0)
    back_n(OUT, 0)
    back_n(OUT, 1)
    for m in range(3):
        ring_send(m, 1)
    back_n(OUT, 2)
    back_x(OUT, 0)
    back_x(OUT, 1)
    back_n(OUT, 3)
    back_x(OUT, 2)
    back_o(OUT, 1)
    back_o(OUT, 2)
    for m in range(3):
        ring_send(m, 2)
    back_x(OUT, 3)
    back_o(OUT, 3)
    back_o(OUT, 0)
    back_n(GRAD, 0)
    back_n(GRAD, 1)
    for m in range(3):
        ring_send(m, 3)
    combine(OUT, o_moe, True)
    back_n(GRAD, 2)
    back_x(GRAD, 0)
    back_x(GRAD, 1)
    back_n(GRAD, 3)
    back_x(GRAD, 2)
    back_o(GRAD, 1)
    back_x(GRAD, 3)
    back_o(GRAD, 2)
    back_o(GRAD, 3)
    back_o(GRAD, 0)
    for m, out in enumerate((o_gate, o_up, o_down)):
        ring_end(m, out)
    combine(GRAD, o_tok, False)
    drain()


def on_device(tokens, expert_ids, gate_values, cotangent, gate_weight, up_weight, down_weight):
    ntok, features = tokens.shape
    depth, units = gate_weight.shape
    nz = lax.axis_size("dp") // 2
    half = features // 2
    rows = 16 * CAP
    slab = (SLAB, half)
    return pl.pallas_call(
        kernel,
        out_shape=(
            jax.ShapeDtypeStruct((ntok, features), BF),
            jax.ShapeDtypeStruct((ntok, features), BF),
            jax.ShapeDtypeStruct((depth, units), F32),
            jax.ShapeDtypeStruct((depth, units), F32),
            jax.ShapeDtypeStruct((depth, units), F32),
        ),
        in_specs=[pl.BlockSpec(memory_space=pltpu.VMEM)] * 7,
        out_specs=(pl.BlockSpec(memory_space=pltpu.VMEM),) * 5,
        scratch_shapes=[
            pltpu.VMEM((2, nz, depth, 3 * units), BF),
            pltpu.VMEM((2, 8) + slab, BF),
            pltpu.VMEM((2, 3) + slab, BF),
            pltpu.VMEM((2, 3) + slab, BF),
            pltpu.VMEM((2, 4) + slab, BF),
            pltpu.VMEM((2, 4) + slab, BF),
            pltpu.VMEM((2, 4) + slab, BF),
            pltpu.VMEM((2, rows, features), BF),
            pltpu.VMEM((2, 4, 4) + slab, BF),
            pltpu.VMEM((2, 4) + slab, BF),
            pltpu.VMEM((2, 4) + slab, BF),
            pltpu.VMEM((2, 4) + slab, BF),
            pltpu.VMEM((2, 8) + slab, BF),
            pltpu.VMEM((nz, depth, 3 * units), BF),
            pltpu.VMEM((21, depth, units), BF),
            pltpu.VMEM((rows, 3 * units), F32),
            pltpu.VMEM((rows, 3 * units), BF),
            pltpu.VMEM((2, ntok, 8 * SLAB), BF),
            pltpu.SemaphoreType.DMA((N_SEM,)),
            pltpu.SemaphoreType.DMA((N_SEM,)),
            pltpu.SemaphoreType.DMA((3,)),
        ],
        compiler_params=pltpu.CompilerParams(
            collective_id=0, has_side_effects=True, vmem_limit_bytes=62 * 1024 * 1024
        ),
        cost_estimate=pl.CostEstimate(
            flops=18 * rows * features * units, bytes_accessed=8 * ntok * features,
            transcendentals=2 * rows * units,
        ),
    )(tokens, expert_ids, gate_values, cotangent, gate_weight, up_weight, down_weight)


def solution(mesh):
    rows, weights = P(("dp", "expert"), None), P("dp", "expert")
    return jax.shard_map(
        on_device,
        mesh=mesh,
        in_specs=(rows, rows, rows, rows, weights, weights, weights),
        out_specs=(rows, rows, weights, weights, weights),
        check_vma=False,
    )
```

```python
import jax
import jax.numpy as jnp
from jax import lax
from jax.experimental import pallas as pl
from jax.experimental.pallas import tpu as pltpu
from jax.sharding import PartitionSpec as P

MESH = pl.DeviceIdType.MESH
BF, F32 = jnp.bfloat16, jnp.float32
HOPS = ({1: 4, -1: 3}, {1: 3, -1: 4}, {1: 4, -1: 3})
OWN, PAR, NBR, FWD = 0, 1, 2, 3
MIRROR = (PAR, OWN, FWD, NBR)
CAP = 24
SLAB = 2 * CAP
BLK = 256
N_SEM = 170


def kernel(
    tok_hbm, ids, gv, cot_hbm, wg, wu, wd,
    o_moe, o_tok, o_gate, o_up, o_down,
    tok, cot, wgr, w_all, dw,
    s_t, own_t, oth_t, par_t, nbr_t, fwd_t, s_c, own_c, oth_c, par_c, nbr_c, fwd_c,
    x_buf, g_buf, x_t, g_t, out_own, out_nbr, out_par, out_fwd, out_oth, out_res,
    part, back_own, back_nbr, back_oth, res, sib_buf, ring_buf,
    pre, act, hid, hid_in, gh_out, gh_in, swap_out, swap_in, sel, ssem, rsem, lsem,
):
    nz = w_all.shape[1]
    units = wg.shape[1]
    half = s_t.shape[-1]
    quarter = half // 2
    rows = x_buf.shape[0]
    group = rows // 4
    ntok = ids.shape[1]
    dp, ex = lax.axis_index("dp"), lax.axis_index("expert")
    z, c = lax.div(dp, 2), lax.rem(dp, 2)
    y, x = lax.div(ex, 4), lax.rem(ex, 4)
    p, hh = lax.div(x, 2), lax.rem(x, 2)
    partner = (dp, ex + 1 - 2 * hh)
    neighbour = (dp, y * 4 + 3 - x)
    sibling = (dp + 1 - 2 * c, ex)
    diagonal = (dp + 1 - 2 * c, ex + 1 - 2 * hh)
    swapped = c != hh

    def zpos(off):
        return lax.rem(z + nz + off, nz)

    def zdev(d):
        return (zpos(d) * 2 + c, ex)

    def ydev(r):
        return (dp, lax.rem(y + r, 4) * 4 + x)

    def expert_at(r, other):
        mine = lax.rem(y + r, 4) * 2 + p
        return mine + (1 - 2 * p) if other else mine

    def cols(m):
        return slice(m * units, (m + 1) * units)

    def block(j):
        return pl.ds(pl.multiple_of(j * BLK, BLK), BLK)

    shards = (wg, wu, wd)
    my_shard = [w_all.at[c, z, :, cols(m)] for m in range(3)]
    load_tok = pltpu.make_async_copy(tok_hbm, tok, lsem.at[0])
    load_cot = pltpu.make_async_copy(cot_hbm, cot, lsem.at[1])
    load_w = [pltpu.make_async_copy(shards[m], my_shard[m], lsem.at[2 + m]) for m in range(3)]
    load_tok.start()
    load_cot.start()

    barrier = pltpu.get_barrier_semaphore()
    for dev in (
        partner, neighbour, sibling, diagonal, zdev(1), zdev(-1), ydev(1), ydev(2), ydev(3)
    ):
        pl.semaphore_signal(barrier, inc=1, device_id=dev, device_id_type=MESH)
    pl.semaphore_wait(barrier, 9)

    copies, received, sent = {}, set(), set()

    def remote(key, src, dst, dev):
        i = len(copies)
        copies[key] = pltpu.make_async_remote_copy(
            src_ref=src, dst_ref=dst, send_sem=ssem.at[i], recv_sem=rsem.at[i],
            device_id=dev, device_id_type=MESH,
        )
        return copies[key]

    def send(key, src, dst, dev):
        remote(key, src, dst, dev).start()

    def got(*key):
        if key not in received:
            received.add(key)
            copies[key].wait_recv()

    def drain(*kinds):
        for key, copy in copies.items():
            if key not in sent and (not kinds or key[0] in kinds):
                sent.add(key)
                copy.wait_send()

    def w_start(m):
        src = shards[m] if m < 2 else my_shard[m]
        for d in (1, -1):
            send(("w", m, d, 1), src, my_shard[m], zdev(d))

    def w_share(m):
        send(("ws", m, 0, 0), shards[m] if m < 2 else my_shard[m], my_shard[m], sibling)

    def w_arrive(m, s):
        for d in (1, -1):
            if s <= HOPS[m][d]:
                got("w", m, d, s)
                piece = w_all.at[c, zpos(-d * s), :, cols(m)]
                if s < HOPS[m][d]:
                    send(("w", m, d, s + 1), piece, piece, zdev(d))
                send(("ws", m, d, s), piece, piece, sibling)

    def w_ready(m):
        for d in (1, -1):
            for s in range(1, HOPS[m][d] + 1):
                got("w", m, d, s)
                got("ws", m, d, s)
        got("ws", m, 0, 0)
        if m < 2:
            load_w[m].wait()

    swap = remote(("swap",), wd, w_all.at[1 - c, z, :, cols(2)], diagonal)
    sent.add(("swap",))
    received.add(("swap",))

    def swap_start():
        @pl.when(swapped)
        def _():
            swap.start()

        @pl.when(jnp.logical_not(swapped))
        def _():
            load_w[2].start()

    def swap_wait():
        @pl.when(swapped)
        def _():
            swap.wait_recv()
            swap.wait_send()

        @pl.when(jnp.logical_not(swapped))
        def _():
            load_w[2].wait()

    def slots():
        lane = lax.broadcasted_iota(jnp.int32, (ntok, ntok), 1)
        down = lax.broadcasted_iota(jnp.int32, (ntok, ntok), 0)
        eye = down == lane
        idv = jnp.sum(
            jnp.where(eye, ids[...].astype(F32), 0.0), axis=1, keepdims=True
        ).astype(jnp.int32)
        gate = jnp.sum(jnp.where(eye, gv[...], 0.0), axis=1, keepdims=True)
        onehot = jnp.where(idv == lane, 1.0, 0.0).astype(F32)
        lower = jnp.where(down > lane, 1.0, 0.0).astype(BF)
        before = jnp.dot(lower, onehot.astype(BF), preferred_element_type=F32)
        order = jnp.sum(before * onehot, axis=1, keepdims=True).astype(jnp.int32)
        place = idv * SLAB + order
        slot = lax.broadcasted_iota(jnp.int32, (ntok, sel.shape[2]), 1)
        for k in range(2):
            sel[k] = jnp.where(slot == place + k * CAP, 1.0, 0.0).astype(BF)
        return gate

    by_rows = (((0,), (0,)), ((), ()))
    by_cols = (((1,), (1,)), ((), ()))

    def spread(k, source, at):
        return lax.dot_general(sel[k], source(at), by_rows, preferred_element_type=F32)

    def dispatch_t():
        def body(j, carry):
            acc = spread(0, lambda at: tok[:, at], block(2 * j))
            acc = acc + spread(1, lambda at: tok[:, at], block(2 * j + 1))
            s_t[:, :, block(j)] = acc.astype(BF).reshape(8, SLAB, BLK)
            return carry

        lax.fori_loop(0, nz, body, 0)

    def dispatch_c(gate):
        def scaled(at):
            return (gate * cot[:, at].astype(F32)).astype(BF)

        def body(j, carry):
            for h in range(2):
                acc = spread(0, scaled, block(2 * j + h))
                acc = acc + spread(1, scaled, block(2 * (j + nz // 2) + h))
                s_c[:, h, :, block(j)] = acc.astype(BF).reshape(8, SLAB, BLK)
            return carry

        lax.fori_loop(0, nz // 2, body, 0)

    stores = {"t": (s_t, own_t, oth_t, par_t, nbr_t, fwd_t), "c": (s_c, own_c, oth_c, par_c, nbr_c, fwd_c)}

    def theirs(ph, ref):
        return ref if ph == "t" else ref.at[1 - hh]

    def y_own(ph, *hops):
        for r in hops:
            s, own = stores[ph][0], stores[ph][1]
            send(("own", ph, r), s.at[expert_at(r, False)], own.at[r - 1], ydev(r))

    def y_oth(ph, *hops):
        for r in hops:
            s, oth = stores[ph][0], stores[ph][2]
            send(("oth", ph, r), s.at[expert_at(r, True)], oth.at[r - 1], ydev(r))

    def self_par(ph):
        s, par = stores[ph][0], stores[ph][3]
        send(("par", ph, 0), theirs(ph, s.at[expert_at(0, False)]), par.at[0], partner)

    def self_nbr(ph):
        s, nbr = stores[ph][0], stores[ph][4]
        send(("nbr", ph, 0), s.at[expert_at(0, True)], nbr.at[0], neighbour)

    def t_own(ph, r):
        got("own", ph, r)
        own, par = stores[ph][1], stores[ph][3]
        send(("par", ph, r), theirs(ph, own.at[r - 1]), par.at[r], partner)

    def t_oth(ph, r):
        got("oth", ph, r)
        oth, nbr = stores[ph][2], stores[ph][4]
        send(("nbr", ph, r), oth.at[r - 1], nbr.at[r], neighbour)

    def t_nbr(ph, r):
        got("nbr", ph, r)
        nbr, fwd = stores[ph][4], stores[ph][5]
        send(("fwd", ph, r), theirs(ph, nbr.at[r]), fwd.at[r], partner)

    wide = 512

    def gather_rows(ph):
        s, own, oth, par, nbr, fwd = stores[ph]
        for r in range(4):
            got("par", ph, r)
            got("fwd", ph, r)

        def slab(g, r, at):
            if g == OWN:
                ref = s.at[expert_at(0, False)] if r == 0 else own.at[r - 1]
            else:
                ref = (None, par, nbr, fwd)[g].at[r]
            if ph == "c" and g in (OWN, NBR):
                ref = ref.at[hh]
            return ref[:, at].astype(F32)

        to_buf, width = (x_buf, half) if ph == "t" else (g_buf, quarter)

        def body(j, carry):
            at = pl.ds(pl.multiple_of(j * wide, wide), wide)
            for g in range(4):
                for r in (0, 2):
                    first, second = slab(g, r, at), slab(g, r + 1, at)
                    base = (g * 4 + r) * CAP
                    for h in range(2):
                        both = jnp.concatenate(
                            [first[h * CAP:(h + 1) * CAP], second[h * CAP:(h + 1) * CAP]], axis=0
                        )
                        to = pl.ds(pl.multiple_of(h * width + j * wide, wide), wide)
                        to_buf[base:base + SLAB, to] = both.astype(BF)
            return carry

        lax.fori_loop(0, width // wide, body, 0)

    def turn(to, source, start, stop):
        def body(j, carry):
            to[block(j), :] = jnp.transpose(source[:, block(j)])
            return carry

        lax.fori_loop(start, stop, body, 0)

    def project_t():
        to = slice(0, 2 * units)
        pre[:, to] = jnp.zeros((rows, 2 * units), F32)

        def body(j, carry):
            acc = None
            for k in range(2):
                term = jnp.dot(
                    x_buf[:, block(k * nz + j)], w_all[k, j, :, to], preferred_element_type=F32
                )
                acc = term if acc is None else acc + term
            pre[:, to] += acc
            return carry

        lax.fori_loop(0, nz, body, 0)

    def project_c():
        pre[:, 2 * units:] = jnp.zeros((rows, 2 * units), F32)

        def body(j, carry):
            for k in range(2):
                acc = None
                for i in range(2):
                    term = jnp.dot(
                        g_buf[:, block(2 * j + i)], w_all[k, 2 * j + i, :, cols(2)],
                        preferred_element_type=F32,
                    )
                    acc = term if acc is None else acc + term
                pre[:, cols(2 + k)] += acc
            return carry

        lax.fori_loop(0, nz // 2, body, 0)

        def pick(at, want):
            low = (want == 0).astype(F32)
            return pre[at, cols(2)] * low + pre[at, cols(3)] * (1.0 - low)

        def split(i, carry):
            at = pl.ds(pl.multiple_of(i * tall, tall), tall)
            gh_out[at, :] = pick(at, 1 - hh).astype(BF)
            pre[at, cols(2)] = pick(at, hh)
            return carry

        lax.fori_loop(0, rows // tall, split, 0)
        send(("gh",), gh_out, gh_in, partner)

    tall = 32

    def activate():
        def body(i, carry):
            at = pl.ds(pl.multiple_of(i * tall, tall), tall)
            gate, up = pre[at, cols(0)], pre[at, cols(1)]
            hid[hh, at, :] = (gate * jax.nn.sigmoid(gate) * up).astype(BF)
            return carry

        lax.fori_loop(0, rows // tall, body, 0)
        send(("hid",), hid.at[hh], hid_in, partner)

    def join_hidden():
        got("hid")
        for g in range(4):
            m = MIRROR[g]
            hid[1 - hh, g * group:(g + 1) * group, :] = hid_in[m * group:(m + 1) * group, :]

    def differentiate():
        got("gh")
        for g in range(4):
            def body(i, carry, g=g):
                at = pl.ds(pl.multiple_of(g * group + i * tall, tall), tall)
                there = pl.ds(pl.multiple_of(MIRROR[g] * group + i * tall, tall), tall)
                gate, up = pre[at, cols(0)], pre[at, cols(1)]
                grad = pre[at, cols(2)] + gh_in[there, :].astype(F32)
                sig = jax.nn.sigmoid(gate)
                act[at, cols(0)] = (grad * up * sig * (1.0 + gate * (1.0 - sig))).astype(BF)
                act[at, cols(1)] = (grad * (gate * sig)).astype(BF)
                return carry

            lax.fori_loop(0, group // tall, body, 0)

    def slabs(first, second):
        shape = (rows // CAP, CAP, BLK)
        joined = jnp.concatenate([first.reshape(shape), second.reshape(shape)], axis=1)
        return joined.astype(BF).reshape(4, 4, SLAB, BLK)

    def outputs():
        def body(j, carry):
            both = []
            for q in range(2):
                value = None
                for k in range(2):
                    term = lax.dot_general(
                        hid[k], w_all[k, j + q * (nz // 2), :, cols(2)], by_cols,
                        preferred_element_type=F32,
                    )
                    value = term if value is None else value + term
                both.append(value)
            joined = slabs(*both)
            out_own[:, hh, :, block(j)] = joined[OWN]
            out_nbr[:, hh, :, block(j)] = joined[NBR]
            out_par[:, :, block(j)] = joined[PAR]
            out_fwd[:, :, block(j)] = joined[FWD]
            return carry

        lax.fori_loop(0, nz // 2, body, 0)

    def row_grads():
        def body(j, carry):
            both = [
                lax.dot_general(
                    act[...], w_all[k, j, :, 0:2 * units], by_cols, preferred_element_type=F32
                )
                for k in range(2)
            ]
            part[:, :, :, block(j)] = slabs(*both)
            return carry

        lax.fori_loop(0, nz, body, 0)

    queue = []
    for turn_of in ("o", "g"):
        for kind in ("bn", "bo"):
            queue += [(kind, turn_of, r) for r in (2, 1, 3, 0)]

    def feed(count):
        for _ in range(count):
            kind, ph, r = queue.pop(0)
            if ph == "o":
                pairs = {"bn": (out_fwd.at[r], out_nbr.at[r, hh]), "bo": (out_par.at[r], out_own.at[r, hh])}
            else:
                pairs = {"bn": (part.at[FWD, r], back_nbr.at[r]), "bo": (part.at[PAR, r], back_own.at[r])}
            send((kind, ph, r), *pairs[kind], partner)

    def add_into(dst, a, b):
        def body(j, carry):
            at = pl.ds(pl.multiple_of(j * wide, wide), wide)
            dst[:, at] = (a[:, at].astype(F32) + b[:, at].astype(F32)).astype(BF)
            return carry

        lax.fori_loop(0, half // wide, body, 0)

    def back_n(ph, r):
        got("bn", ph, r)
        if ph == "o":
            mine, oth = out_nbr.at[r], out_oth
        else:
            mine, oth = part.at[NBR, r], back_oth
            add_into(mine, mine, back_nbr.at[r])
        send(("bx", ph, r), mine, oth.at[r], neighbour)

    def back_o(ph, r):
        got("bo", ph, r)
        e = expert_at(0, False)
        if ph == "o":
            mine, to = out_own.at[r], out_res.at[e]
            if r == 0:
                out_res[e] = out_own[0]
        else:
            mine, to = part.at[OWN, r], res.at[e]
            add_into(to if r == 0 else mine, mine, back_own.at[r])
        if r > 0:
            send(("ro", ph, r), mine, to, ydev(4 - r))

    def back_x(ph, r):
        got("bx", ph, r)
        e = expert_at(0, True)
        oth, to = (out_oth, out_res) if ph == "o" else (back_oth, res)
        if r == 0:
            to[e] = oth[0]
        else:
            send(("rx", ph, r), oth.at[r], to.at[e], ydev(4 - r))

    def combine_o(gate):
        for r in (1, 2, 3):
            got("ro", "o", r)
            got("rx", "o", r)

        def body(j, carry):
            for h in range(2):
                back = out_res[:, h, :, block(j)].reshape(8 * SLAB, BLK)
                for q in range(2):
                    value = gate * jnp.dot(sel[q], back, preferred_element_type=F32)
                    tok[:, block(2 * (j + q * (nz // 2)) + h)] = value.astype(BF)
            return carry

        lax.fori_loop(0, nz // 2, body, 0)
        store(0, tok, o_moe)

    def combine_g():
        for r in (1, 2, 3):
            got("ro", "g", r)
            got("rx", "g", r)

        def body(j, carry):
            back = res[:, :, block(j)].reshape(8 * SLAB, BLK)
            for h in range(2):
                value = jnp.dot(sel[h], back, preferred_element_type=F32)
                cot[:, block(2 * j + h)] = value.astype(BF)
            return carry

        lax.fori_loop(0, nz, body, 0)
        store(1, cot, o_tok)

    def grad_at(m, k, zz):
        ref = w_all if m == 2 else dw
        return ref.at[k, zz, :, cols(m)]

    ORDER = (4, 3, 5, 2, 6, 1, 7, 0)

    def offset(j):
        odd = lax.rem(j, 2)
        return 4 + lax.div(j, 2) * (1 - odd) - lax.div(j + 1, 2) * odd

    def weight_grads(kind, k, to_sibling):
        to, at_cols = (w_all, cols(2)) if kind == "d" else (dw, slice(0, 2 * units))
        base = len(copies)

        def piece(j, off):
            return pltpu.make_async_remote_copy(
                src_ref=to.at[k, zpos(off), :, at_cols], dst_ref=sib_buf.at[off, :, at_cols],
                send_sem=ssem.at[base + j], recv_sem=rsem.at[base + j],
                device_id=sibling, device_id_type=MESH,
            )

        def body(j, carry):
            off = offset(j)
            zz = zpos(off)
            if kind == "d":
                value = jnp.dot(g_t[block(zz), :], hid[k], preferred_element_type=F32)
            else:
                value = jnp.dot(
                    x_t[block(k * nz + zz), :], act[...], preferred_element_type=F32
                )
            to[k, zz, :, at_cols] = value.astype(BF)
            if to_sibling:
                piece(j, off).start()
            return carry

        lax.fori_loop(0, nz, body, 0)
        if to_sibling:
            for j, off in enumerate(ORDER):
                copies["sib", kind, off] = piece(j, off)

    ring_slots = {}

    def slot_of(*key):
        return ring_buf.at[ring_slots.setdefault(key, len(ring_slots))]

    def local_sum(m, off):
        got("sib", "d" if m == 2 else "gu", off)
        mine = grad_at(m, c, zpos(off))
        return mine[...].astype(F32) + sib_buf[off, :, cols(m)].astype(F32)

    def ring_send(m, s):
        for d in (1, -1):
            hops = HOPS[m][d]
            if s < hops:
                off = (d * (hops - s)) % nz
                total = local_sum(m, off)
                if s > 0:
                    got("ring", m, d, s - 1)
                    total = total + slot_of(m, d, s - 1)[...].astype(F32)
                piece = grad_at(m, c, zpos(off))
                piece[...] = total.astype(BF)
                send(("ring", m, d, s), piece, slot_of(m, d, s), zdev(d))

    def ring_total(m):
        total = local_sum(m, 0)
        for d in (1, -1):
            last = HOPS[m][d] - 1
            got("ring", m, d, last)
            total = total + slot_of(m, d, last)[...].astype(F32)
        return total

    def ring_end(m):
        wgr[m] = ring_total(m)
        store(2 + m, wgr.at[m], (o_gate, o_up)[m])

    def ring_end_down():
        wgr[2] = ring_total(2)
        back = remote(("back",), swap_out, swap_in, diagonal)
        sent.add(("back",))
        received.add(("back",))

        @pl.when(swapped)
        def _():
            swap_out[...] = wgr[2].astype(BF)
            back.start()

        return back

    def down_done(back):
        @pl.when(swapped)
        def _():
            back.wait_recv()
            back.wait_send()
            wgr[2] = swap_in[...].astype(F32)

        store(4, wgr.at[2], o_down)

    stored = []

    def store(i, src, dst):
        stored.append(pltpu.make_async_copy(src, dst, lsem.at[5 + i]))
        stored[-1].start()

    def ring(*steps):
        for m, s in steps:
            ring_send(m, s)

    w_start(0)
    w_start(1)
    swap_start()
    w_share(0)
    w_share(1)
    load_w[0].start()
    load_w[1].start()
    gate_col = slots()
    load_tok.wait()
    dispatch_t()
    self_par("t")
    self_nbr("t")
    y_own("t", 1, 3)
    load_cot.wait()
    dispatch_c(gate_col)
    t_own("t", 1)
    t_own("t", 3)
    y_oth("t", 1, 3, 2)
    t_nbr("t", 0)
    w_arrive(0, 1)
    w_arrive(1, 1)
    t_oth("t", 1)
    t_oth("t", 3)
    y_own("t", 2)
    w_arrive(0, 2)
    t_oth("t", 2)
    t_nbr("t", 1)
    w_arrive(1, 2)
    t_nbr("t", 3)
    t_own("t", 2)
    y_own("c", 1, 3)
    w_arrive(0, 3)
    self_nbr("c")
    t_nbr("t", 2)
    w_arrive(1, 3)
    swap_wait()
    w_start(2)
    w_share(2)
    y_oth("c", 1, 3, 2)
    self_par("c")
    w_arrive(0, 4)
    w_arrive(1, 4)
    t_own("c", 1)
    t_own("c", 3)
    t_oth("c", 1)
    t_oth("c", 3)
    y_own("c", 2)
    t_nbr("c", 0)
    gather_rows("t")
    w_arrive(2, 1)
    t_oth("c", 2)
    w_ready(0)
    w_ready(1)
    project_t()
    activate()
    t_own("c", 2)
    t_nbr("c", 1)
    t_nbr("c", 3)
    w_arrive(2, 2)
    t_nbr("c", 2)
    turn(x_t, x_buf, 0, nz)
    w_arrive(2, 3)
    turn(x_t, x_buf, nz, 2 * nz)
    w_arrive(2, 4)
    w_ready(2)
    gather_rows("c")
    project_c()
    drain("w", "ws")
    turn(g_t, g_buf, 0, nz)
    join_hidden()
    outputs()
    weight_grads("d", 1 - c, True)
    weight_grads("d", c, False)
    ring((2, 0))
    got("gh")
    feed(5)
    differentiate()
    weight_grads("gu", 1 - c, True)
    ring((2, 1))
    back_n("o", 2)
    back_n("o", 1)
    weight_grads("gu", c, False)
    ring((0, 0), (1, 0))
    feed(3)
    row_grads()
    feed(2)
    back_n("o", 3)
    back_n("o", 0)
    ring((2, 2))
    back_x("o", 2)
    back_x("o", 1)
    back_o("o", 2)
    back_o("o", 1)
    back_o("o", 3)
    back_x("o", 3)
    ring((0, 1), (1, 1))
    feed(1)
    back_o("o", 0)
    back_x("o", 0)
    back_n("g", 2)
    feed(1)
    ring((2, 3))
    back_n("g", 1)
    feed(1)
    back_x("g", 2)
    ring((0, 2), (1, 2))
    back_n("g", 3)
    feed(1)
    back_x("g", 1)
    combine_o(gate_col)
    back_n("g", 0)
    feed(1)
    back_x("g", 3)
    swapping = ring_end_down()
    back_o("g", 2)
    feed(1)
    back_x("g", 0)
    ring((0, 3), (1, 3))
    back_o("g", 1)
    down_done(swapping)
    back_o("g", 3)
    ring_end(0)
    ring_end(1)
    back_o("g", 0)
    combine_g()
    drain()
    for copy in stored:
        copy.wait()


def finish(*refs):
    ins, outs, held, sems = refs[0:5], refs[5:10], refs[10:15], refs[15]
    loads = [pltpu.make_async_copy(a, b, sems.at[i]) for i, (a, b) in enumerate(zip(ins, held))]
    moves = [pltpu.make_async_copy(a, b, sems.at[5 + i]) for i, (a, b) in enumerate(zip(held, outs))]
    for load in loads:
        load.start()
    for load, move in zip(loads, moves):
        load.wait()
        move.start()
    for move in moves:
        move.wait()


def on_device(tokens, expert_ids, gate_values, cotangent, gate_weight, up_weight, down_weight):
    ntok, features = tokens.shape
    depth, units = gate_weight.shape
    nz = lax.axis_size("dp") // 2
    half = features // 2
    rows = 16 * CAP
    slab = (SLAB, half)
    small = (SLAB, half // 2)
    pair = (2,) + small
    shapes = (
        jax.ShapeDtypeStruct((ntok, features), BF),
        jax.ShapeDtypeStruct((ntok, features), BF),
        jax.ShapeDtypeStruct((depth, units), F32),
        jax.ShapeDtypeStruct((depth, units), F32),
        jax.ShapeDtypeStruct((depth, units), F32),
    )
    hbm, vmem = pl.BlockSpec(memory_space=pl.ANY), pl.BlockSpec(memory_space=pltpu.VMEM)
    results = pl.pallas_call(
        kernel,
        out_shape=shapes,
        in_specs=[hbm, vmem, vmem, hbm, hbm, hbm, hbm],
        out_specs=(hbm,) * 5,
        scratch_shapes=[
            pltpu.VMEM((ntok, features), BF),
            pltpu.VMEM((ntok, features), BF),
            pltpu.VMEM((3, depth, units), F32),
            pltpu.VMEM((2, nz, depth, 3 * units), BF),
            pltpu.VMEM((2, nz, depth, 2 * units), BF),
            pltpu.VMEM((8,) + slab, BF),
            pltpu.VMEM((3,) + slab, BF),
            pltpu.VMEM((3,) + slab, BF),
            pltpu.VMEM((4,) + slab, BF),
            pltpu.VMEM((4,) + slab, BF),
            pltpu.VMEM((4,) + slab, BF),
            pltpu.VMEM((8,) + pair, BF),
            pltpu.VMEM((3,) + pair, BF),
            pltpu.VMEM((3,) + pair, BF),
            pltpu.VMEM((4,) + small, BF),
            pltpu.VMEM((4,) + pair, BF),
            pltpu.VMEM((4,) + small, BF),
            pltpu.VMEM((rows, features), BF),
            pltpu.VMEM((rows, half), BF),
            pltpu.VMEM((features, rows), BF),
            pltpu.VMEM((half, rows), BF),
            pltpu.VMEM((4,) + pair, BF),
            pltpu.VMEM((4,) + pair, BF),
            pltpu.VMEM((4,) + small, BF),
            pltpu.VMEM((4,) + small, BF),
            pltpu.VMEM((4,) + pair, BF),
            pltpu.VMEM((8,) + pair, BF),
            pltpu.VMEM((4, 4) + slab, BF),
            pltpu.VMEM((4,) + slab, BF),
            pltpu.VMEM((4,) + slab, BF),
            pltpu.VMEM((4,) + slab, BF),
            pltpu.VMEM((8,) + slab, BF),
            pltpu.VMEM((nz, depth, 3 * units), BF),
            pltpu.VMEM((21, depth, units), BF),
            pltpu.VMEM((rows, 4 * units), F32),
            pltpu.VMEM((rows, 2 * units), BF),
            pltpu.VMEM((2, rows, units), BF),
            pltpu.VMEM((rows, units), BF),
            pltpu.VMEM((rows, units), BF),
            pltpu.VMEM((rows, units), BF),
            pltpu.VMEM((depth, units), BF),
            pltpu.VMEM((depth, units), BF),
            pltpu.VMEM((2, ntok, 8 * SLAB), BF),
            pltpu.SemaphoreType.DMA((N_SEM,)),
            pltpu.SemaphoreType.DMA((N_SEM,)),
            pltpu.SemaphoreType.DMA((10,)),
        ],
        compiler_params=pltpu.CompilerParams(
            collective_id=0, has_side_effects=True, vmem_limit_bytes=62 * 1024 * 1024
        ),
        cost_estimate=pl.CostEstimate(
            flops=18 * rows * features * units, bytes_accessed=8 * ntok * features,
            transcendentals=2 * rows * units,
        ),
    )(
        tokens, expert_ids.reshape(1, ntok), gate_values.reshape(1, ntok), cotangent,
        gate_weight, up_weight, down_weight,
    )
    return pl.pallas_call(
        finish,
        out_shape=shapes,
        in_specs=[hbm] * 5,
        out_specs=(hbm,) * 5,
        scratch_shapes=[pltpu.VMEM(a.shape, a.dtype) for a in shapes]
        + [pltpu.SemaphoreType.DMA((10,))],
        compiler_params=pltpu.CompilerParams(vmem_limit_bytes=62 * 1024 * 1024),
    )(*results)


def solution(mesh):
    rows, weights = P(("dp", "expert"), None), P("dp", "expert")
    return jax.shard_map(
        on_device,
        mesh=mesh,
        in_specs=(rows, rows, rows, rows, weights, weights, weights),
        out_specs=(rows, rows, weights, weights, weights),
        check_vma=False,
    )
```

```python
import math

import jax
import jax.numpy as jnp
from jax import lax
from jax.experimental import pallas as pl
from jax.experimental.pallas import tpu as pltpu
from jax.sharding import PartitionSpec as P

MESH = pl.DeviceIdType.MESH
BF, F32 = jnp.bfloat16, jnp.float32
HOPS = ({1: 4, -1: 3}, {1: 3, -1: 4}, {1: 4, -1: 3})
OWN, PAR, NBR, FWD = 0, 1, 2, 3
MIRROR = (PAR, OWN, FWD, NBR)
CAP = 24
SLAB = 2 * CAP
BLK = 256
N_SEND, N_RECV = 14, 123


def kernel(
    tok_hbm, ids, gv, cot_hbm, wg, wu, wd,
    o_moe, o_res, o_sel, o_gate, o_up, o_down,
    tok, cot, w_all, dw,
    s_t, own_t, oth_t, par_t, nbr_t, fwd_t, s_c, own_c, oth_c, par_c, nbr_c, fwd_c,
    x_buf, g_buf, x_t, g_t, out_own, out_nbr, out_par, out_fwd, out_oth, out_res,
    part, back_own, back_nbr, back_oth, res, sib_buf, ring_buf,
    pre, act, hid, hid_in, gh_out, gh_in, swap_out, swap_in, sel, sel_t, ssem, rsem, lsem,
):
    nz = w_all.shape[1]
    units = wg.shape[1]
    half = s_t.shape[-1]
    quarter = half // 2
    rows = x_buf.shape[0]
    group = rows // 4
    ntok = ids.shape[1]
    dp, ex = lax.axis_index("dp"), lax.axis_index("expert")
    z, c = lax.div(dp, 2), lax.rem(dp, 2)
    y, x = lax.div(ex, 4), lax.rem(ex, 4)
    p, hh = lax.div(x, 2), lax.rem(x, 2)
    partner = (dp, ex + 1 - 2 * hh)
    neighbour = (dp, y * 4 + 3 - x)
    sibling = (dp + 1 - 2 * c, ex)
    diagonal = (dp + 1 - 2 * c, ex + 1 - 2 * hh)
    swapped = c != hh

    def zpos(off):
        return lax.rem(z + nz + off, nz)

    def zdev(d):
        return (zpos(d) * 2 + c, ex)

    def ydev(r):
        return (dp, lax.rem(y + r, 4) * 4 + x)

    def expert_at(r, other):
        mine = lax.rem(y + r, 4) * 2 + p
        return mine + (1 - 2 * p) if other else mine

    def cols(m):
        return slice(m * units, (m + 1) * units)

    def block(j):
        return pl.ds(pl.multiple_of(j * BLK, BLK), BLK)

    shards = (wg, wu, wd)
    my_shard = [w_all.at[c, z, :, cols(m)] for m in range(3)]
    load_tok = pltpu.make_async_copy(tok_hbm, tok, lsem.at[0])
    load_cot = pltpu.make_async_copy(cot_hbm, cot, lsem.at[1])
    load_w = [pltpu.make_async_copy(shards[m], my_shard[m], lsem.at[2 + m]) for m in range(3)]
    load_tok.start()
    load_cot.start()

    barrier = pltpu.get_barrier_semaphore()
    for dev in (
        partner, neighbour, sibling, diagonal, zdev(1), zdev(-1), ydev(1), ydev(2), ydev(3)
    ):
        pl.semaphore_signal(barrier, inc=1, device_id=dev, device_id_type=MESH)
    pl.semaphore_wait(barrier, 9)

    copies, sizes, received, sent = {}, {}, set(), set()
    send_slots, recv_slots = {}, {}

    def send_group(key):
        if key[0] in ("own", "oth", "par", "nbr", "fwd"):
            return ("rows", key[1])
        if key[0] in ("bn", "bo", "bx", "ro", "rx"):
            return ("back", key[1])
        if key[0] in ("hid", "gh"):
            return ("units",)
        return key[:2] if key[0] in ("ws", "sib") else key[:1]

    def recv_group(key):
        if key[0] in ("par", "fwd"):
            return ("pair", key[1])
        return key[:2] if key[0] == "ws" else key

    def numbered(slots, name):
        return slots.setdefault(name, len(slots))

    def remote(key, src, dst, dev):
        i, j = numbered(send_slots, send_group(key)), numbered(recv_slots, recv_group(key))
        copies[key] = pltpu.make_async_remote_copy(
            src_ref=src, dst_ref=dst, send_sem=ssem.at[i], recv_sem=rsem.at[j],
            device_id=dev, device_id_type=MESH,
        )
        sizes[key] = src.shape
        return copies[key]

    def send(key, src, dst, dev):
        remote(key, src, dst, dev).start()

    piece_size = math.prod(ring_buf.shape[1:])

    def together(keys, i, j):
        total = sum(math.prod(sizes[k]) for k in keys)
        assert total % piece_size == 0
        ref = ring_buf.at[0:total // piece_size]
        return pltpu.make_async_remote_copy(
            src_ref=ref, dst_ref=ref, send_sem=ssem.at[i], recv_sem=rsem.at[j],
            device_id=partner, device_id_type=MESH,
        )

    def got(*key):
        name = recv_group(key)
        if name not in received:
            received.add(name)
            keys = [k for k in copies if recv_group(k) == name]
            if len(keys) == 1:
                copies[key].wait_recv()
            else:
                together(keys, 0, recv_slots[name]).wait_recv()

    def drain(*kinds):
        for name in send_slots:
            if name not in sent and (not kinds or name[0] in kinds):
                sent.add(name)
                keys = [k for k in copies if send_group(k) == name]
                together(keys, send_slots[name], 0).wait_send()

    def w_start(m):
        src = shards[m] if m < 2 else my_shard[m]
        for d in (1, -1):
            send(("w", m, d, 1), src, my_shard[m], zdev(d))

    def w_share(m):
        send(("ws", m, 0, 0), shards[m] if m < 2 else my_shard[m], my_shard[m], sibling)

    def w_arrive(m, s):
        for d in (1, -1):
            if s <= HOPS[m][d]:
                got("w", m, d, s)
                piece = w_all.at[c, zpos(-d * s), :, cols(m)]
                if s < HOPS[m][d]:
                    send(("w", m, d, s + 1), piece, piece, zdev(d))
                send(("ws", m, d, s), piece, piece, sibling)

    def w_ready(m):
        for d in (1, -1):
            for s in range(1, HOPS[m][d] + 1):
                got("w", m, d, s)
                got("ws", m, d, s)
        got("ws", m, 0, 0)
        if m < 2:
            load_w[m].wait()

    swap = remote(("swap",), wd, w_all.at[1 - c, z, :, cols(2)], diagonal)
    sent.add(("swap",))
    received.add(("swap",))

    def swap_start():
        @pl.when(swapped)
        def _():
            swap.start()

        @pl.when(jnp.logical_not(swapped))
        def _():
            load_w[2].start()

    def swap_wait():
        @pl.when(swapped)
        def _():
            swap.wait_recv()
            swap.wait_send()

        @pl.when(jnp.logical_not(swapped))
        def _():
            load_w[2].wait()

    stored = []

    def store(i, src, dst):
        stored.append(pltpu.make_async_copy(src, dst, lsem.at[5 + i]))
        stored[-1].start()

    def slots():
        lane = lax.broadcasted_iota(jnp.int32, (ntok, ntok), 1)
        down = lax.broadcasted_iota(jnp.int32, (ntok, ntok), 0)
        eye = down == lane
        idv = jnp.sum(
            jnp.where(eye, ids[...].astype(F32), 0.0), axis=1, keepdims=True
        ).astype(jnp.int32)
        gate = jnp.sum(jnp.where(eye, gv[...], 0.0), axis=1, keepdims=True)
        onehot = jnp.where(idv == lane, 1.0, 0.0).astype(F32)
        lower = jnp.where(down > lane, 1.0, 0.0).astype(BF)
        before = jnp.dot(lower, onehot.astype(BF), preferred_element_type=F32)
        order = jnp.sum(before * onehot, axis=1, keepdims=True).astype(jnp.int32)
        place = idv * SLAB + order
        slot = lax.broadcasted_iota(jnp.int32, (ntok, sel.shape[2]), 1)
        for k in range(2):
            chosen = jnp.where(slot == place + k * CAP, 1.0, 0.0)
            sel[k] = chosen.astype(BF)
            sel_t[k] = jnp.transpose(chosen).astype(BF)
        store(1, sel, o_sel)
        return gate

    by_cols = (((1,), (1,)), ((), ()))

    def spread(k, source, at):
        return jnp.dot(sel_t[k], source(at), preferred_element_type=F32)

    def dispatch_t():
        def body(j, carry):
            acc = spread(0, lambda at: tok[:, at], block(2 * j))
            acc = acc + spread(1, lambda at: tok[:, at], block(2 * j + 1))
            s_t[:, :, block(j)] = acc.astype(BF).reshape(8, SLAB, BLK)
            return carry

        lax.fori_loop(0, nz, body, 0)

    def dispatch_c(gate):
        def scaled(at):
            return (gate * cot[:, at].astype(F32)).astype(BF)

        def body(j, carry):
            for h in range(2):
                acc = spread(0, scaled, block(2 * j + h))
                acc = acc + spread(1, scaled, block(2 * (j + nz // 2) + h))
                s_c[:, h, :, block(j)] = acc.astype(BF).reshape(8, SLAB, BLK)
            return carry

        lax.fori_loop(0, nz // 2, body, 0)

    stores = {"t": (s_t, own_t, oth_t, par_t, nbr_t, fwd_t), "c": (s_c, own_c, oth_c, par_c, nbr_c, fwd_c)}

    def theirs(ph, ref):
        return ref if ph == "t" else ref.at[1 - hh]

    def y_own(ph, *hops):
        for r in hops:
            s, own = stores[ph][0], stores[ph][1]
            send(("own", ph, r), s.at[expert_at(r, False)], own.at[r - 1], ydev(r))

    def y_oth(ph, *hops):
        for r in hops:
            s, oth = stores[ph][0], stores[ph][2]
            send(("oth", ph, r), s.at[expert_at(r, True)], oth.at[r - 1], ydev(r))

    def self_par(ph):
        s, par = stores[ph][0], stores[ph][3]
        send(("par", ph, 0), theirs(ph, s.at[expert_at(0, False)]), par.at[0], partner)

    def self_nbr(ph):
        s, nbr = stores[ph][0], stores[ph][4]
        send(("nbr", ph, 0), s.at[expert_at(0, True)], nbr.at[0], neighbour)

    def t_own(ph, r):
        got("own", ph, r)
        own, par = stores[ph][1], stores[ph][3]
        send(("par", ph, r), theirs(ph, own.at[r - 1]), par.at[r], partner)

    def t_oth(ph, r):
        got("oth", ph, r)
        oth, nbr = stores[ph][2], stores[ph][4]
        send(("nbr", ph, r), oth.at[r - 1], nbr.at[r], neighbour)

    def t_nbr(ph, r):
        got("nbr", ph, r)
        nbr, fwd = stores[ph][4], stores[ph][5]
        send(("fwd", ph, r), theirs(ph, nbr.at[r]), fwd.at[r], partner)

    wide = 512

    def gather_rows(ph):
        s, own, oth, par, nbr, fwd = stores[ph]
        for r in range(4):
            got("par", ph, r)
            got("fwd", ph, r)

        def slab(g, r, at):
            if g == OWN:
                ref = s.at[expert_at(0, False)] if r == 0 else own.at[r - 1]
            else:
                ref = (None, par, nbr, fwd)[g].at[r]
            if ph == "c" and g in (OWN, NBR):
                ref = ref.at[hh]
            return ref[:, at].astype(F32)

        to_buf, width = (x_buf, half) if ph == "t" else (g_buf, quarter)

        def body(j, carry):
            at = pl.ds(pl.multiple_of(j * wide, wide), wide)
            for g in range(4):
                for r in (0, 2):
                    first, second = slab(g, r, at), slab(g, r + 1, at)
                    base = (g * 4 + r) * CAP
                    for h in range(2):
                        both = jnp.concatenate(
                            [first[h * CAP:(h + 1) * CAP], second[h * CAP:(h + 1) * CAP]], axis=0
                        )
                        to = pl.ds(pl.multiple_of(h * width + j * wide, wide), wide)
                        to_buf[base:base + SLAB, to] = both.astype(BF)
            return carry

        lax.fori_loop(0, width // wide, body, 0)

    def turn(to, source, start, stop):
        def body(j, carry):
            to[block(j), :] = jnp.transpose(source[:, block(j)])
            return carry

        lax.fori_loop(start, stop, body, 0)

    def project_t():
        to = slice(0, 2 * units)
        pre[:, to] = jnp.zeros((rows, 2 * units), F32)

        def body(j, carry):
            acc = None
            for k in range(2):
                term = jnp.dot(
                    x_buf[:, block(k * nz + j)], w_all[k, j, :, to], preferred_element_type=F32
                )
                acc = term if acc is None else acc + term
            pre[:, to] += acc
            return carry

        lax.fori_loop(0, nz, body, 0)

    def project_c():
        pre[:, 2 * units:] = jnp.zeros((rows, 2 * units), F32)

        def body(j, carry):
            for k in range(2):
                acc = None
                for i in range(2):
                    term = jnp.dot(
                        g_buf[:, block(2 * j + i)], w_all[k, 2 * j + i, :, cols(2)],
                        preferred_element_type=F32,
                    )
                    acc = term if acc is None else acc + term
                pre[:, cols(2 + k)] += acc
            return carry

        lax.fori_loop(0, nz // 2, body, 0)

        def pick(at, want):
            low = (want == 0).astype(F32)
            return pre[at, cols(2)] * low + pre[at, cols(3)] * (1.0 - low)

        def split(i, carry):
            at = pl.ds(pl.multiple_of(i * tall, tall), tall)
            gh_out[at, :] = pick(at, 1 - hh).astype(BF)
            pre[at, cols(2)] = pick(at, hh)
            return carry

        lax.fori_loop(0, rows // tall, split, 0)
        send(("gh",), gh_out, gh_in, partner)

    tall = 32

    def activate():
        def body(i, carry):
            at = pl.ds(pl.multiple_of(i * tall, tall), tall)
            gate, up = pre[at, cols(0)], pre[at, cols(1)]
            hid[hh, at, :] = (gate * jax.nn.sigmoid(gate) * up).astype(BF)
            return carry

        lax.fori_loop(0, rows // tall, body, 0)
        send(("hid",), hid.at[hh], hid_in, partner)

    def join_hidden():
        got("hid")
        for g in range(4):
            m = MIRROR[g]
            hid[1 - hh, g * group:(g + 1) * group, :] = hid_in[m * group:(m + 1) * group, :]

    def differentiate():
        got("gh")
        for g in range(4):
            def body(i, carry, g=g):
                at = pl.ds(pl.multiple_of(g * group + i * tall, tall), tall)
                there = pl.ds(pl.multiple_of(MIRROR[g] * group + i * tall, tall), tall)
                gate, up = pre[at, cols(0)], pre[at, cols(1)]
                grad = pre[at, cols(2)] + gh_in[there, :].astype(F32)
                sig = jax.nn.sigmoid(gate)
                act[at, cols(0)] = (grad * up * sig * (1.0 + gate * (1.0 - sig))).astype(BF)
                act[at, cols(1)] = (grad * (gate * sig)).astype(BF)
                return carry

            lax.fori_loop(0, group // tall, body, 0)

    def slabs(first, second):
        shape = (rows // CAP, CAP, BLK)
        joined = jnp.concatenate([first.reshape(shape), second.reshape(shape)], axis=1)
        return joined.astype(BF).reshape(4, 4, SLAB, BLK)

    def outputs():
        def body(j, carry):
            both = []
            for q in range(2):
                value = None
                for k in range(2):
                    term = lax.dot_general(
                        hid[k], w_all[k, j + q * (nz // 2), :, cols(2)], by_cols,
                        preferred_element_type=F32,
                    )
                    value = term if value is None else value + term
                both.append(value)
            joined = slabs(*both)
            out_own[:, hh, :, block(j)] = joined[OWN]
            out_nbr[:, hh, :, block(j)] = joined[NBR]
            out_par[:, :, block(j)] = joined[PAR]
            out_fwd[:, :, block(j)] = joined[FWD]
            return carry

        lax.fori_loop(0, nz // 2, body, 0)

    def row_grads():
        def body(j, carry):
            both = [
                lax.dot_general(
                    act[...], w_all[k, j, :, 0:2 * units], by_cols, preferred_element_type=F32
                )
                for k in range(2)
            ]
            part[:, :, :, block(j)] = slabs(*both)
            return carry

        lax.fori_loop(0, nz, body, 0)

    queue = []
    for turn_of in ("o", "g"):
        for kind in ("bn", "bo"):
            queue += [(kind, turn_of, r) for r in (2, 1, 3, 0)]

    def feed(count):
        for _ in range(count):
            kind, ph, r = queue.pop(0)
            if ph == "o":
                pairs = {"bn": (out_fwd.at[r], out_nbr.at[r, hh]), "bo": (out_par.at[r], out_own.at[r, hh])}
            else:
                pairs = {"bn": (part.at[FWD, r], back_nbr.at[r]), "bo": (part.at[PAR, r], back_own.at[r])}
            send((kind, ph, r), *pairs[kind], partner)

    def add_into(dst, a, b):
        def body(j, carry):
            at = pl.ds(pl.multiple_of(j * wide, wide), wide)
            dst[:, at] = (a[:, at].astype(F32) + b[:, at].astype(F32)).astype(BF)
            return carry

        lax.fori_loop(0, half // wide, body, 0)

    def back_n(ph, r):
        got("bn", ph, r)
        if ph == "o":
            mine, oth = out_nbr.at[r], out_oth
        else:
            mine, oth = part.at[NBR, r], back_oth
            add_into(mine, mine, back_nbr.at[r])
        send(("bx", ph, r), mine, oth.at[r], neighbour)

    def back_o(ph, r):
        got("bo", ph, r)
        e = expert_at(0, False)
        if ph == "o":
            mine, to = out_own.at[r], out_res.at[e]
            if r == 0:
                out_res[e] = out_own[0]
        else:
            mine, to = part.at[OWN, r], res.at[e]
            add_into(to if r == 0 else mine, mine, back_own.at[r])
        if r > 0:
            send(("ro", ph, r), mine, to, ydev(4 - r))

    def back_x(ph, r):
        got("bx", ph, r)
        e = expert_at(0, True)
        oth, to = (out_oth, out_res) if ph == "o" else (back_oth, res)
        if r == 0:
            to[e] = oth[0]
        else:
            send(("rx", ph, r), oth.at[r], to.at[e], ydev(4 - r))

    def combine_o(gate):
        for r in (1, 2, 3):
            got("ro", "o", r)
            got("rx", "o", r)

        def body(j, carry):
            for h in range(2):
                back = out_res[:, h, :, block(j)].reshape(8 * SLAB, BLK)
                for q in range(2):
                    value = gate * jnp.dot(sel[q], back, preferred_element_type=F32)
                    tok[:, block(2 * (j + q * (nz // 2)) + h)] = value.astype(BF)
            return carry

        lax.fori_loop(0, nz // 2, body, 0)
        store(0, tok, o_moe)

    def res_out(r):
        for i, other in enumerate((False, True)):
            if r > 0:
                got("rx" if other else "ro", "g", r)
            e = expert_at(r, other)
            store(5 + 2 * r + i, res.at[e], o_res.at[e])

    def grad_at(m, k, zz):
        ref = w_all if m == 2 else dw
        return ref.at[k, zz, :, cols(m)]

    ORDER = (4, 3, 5, 2, 6, 1, 7, 0)

    def offset(j):
        odd = lax.rem(j, 2)
        return 4 + lax.div(j, 2) * (1 - odd) - lax.div(j + 1, 2) * odd

    def weight_grads(kind, k, to_sibling):
        base = len(recv_slots)
        to, at_cols = (w_all, cols(2)) if kind == "d" else (dw, slice(0, 2 * units))
        if to_sibling:
            first = numbered(send_slots, ("sib", kind))

        def piece(j, off):
            return pltpu.make_async_remote_copy(
                src_ref=to.at[k, zpos(off), :, at_cols], dst_ref=sib_buf.at[off, :, at_cols],
                send_sem=ssem.at[first], recv_sem=rsem.at[base + j],
                device_id=sibling, device_id_type=MESH,
            )

        def body(j, carry):
            off = offset(j)
            zz = zpos(off)
            if kind == "d":
                value = jnp.dot(g_t[block(zz), :], hid[k], preferred_element_type=F32)
            else:
                value = jnp.dot(
                    x_t[block(k * nz + zz), :], act[...], preferred_element_type=F32
                )
            to[k, zz, :, at_cols] = value.astype(BF)
            if to_sibling:
                piece(j, off).start()
            return carry

        lax.fori_loop(0, nz, body, 0)
        if to_sibling:
            for j, off in enumerate(ORDER):
                key = ("sib", kind, off)
                numbered(recv_slots, key)
                copies[key] = piece(j, off)
                sizes[key] = (w_all.shape[2], units if kind == "d" else 2 * units)

    ring_slots = {}

    def slot_of(*key):
        return ring_buf.at[ring_slots.setdefault(key, len(ring_slots))]

    def local_sum(m, off):
        got("sib", "d" if m == 2 else "gu", off)
        mine = grad_at(m, c, zpos(off))
        return mine[...].astype(F32) + sib_buf[off, :, cols(m)].astype(F32)

    def ring_send(m, s):
        for d in (1, -1):
            hops = HOPS[m][d]
            if s < hops:
                off = (d * (hops - s)) % nz
                total = local_sum(m, off)
                if s > 0:
                    got("ring", m, d, s - 1)
                    total = total + slot_of(m, d, s - 1)[...].astype(F32)
                piece = grad_at(m, c, zpos(off))
                piece[...] = total.astype(BF)
                send(("ring", m, d, s), piece, slot_of(m, d, s), zdev(d))

    def ring_total(m):
        total = local_sum(m, 0)
        for d in (1, -1):
            last = HOPS[m][d] - 1
            got("ring", m, d, last)
            total = total + slot_of(m, d, last)[...].astype(F32)
        return total

    def done(m):
        return pre.at[0:w_all.shape[2], cols(m)]

    def ring_end(m):
        done(m)[...] = ring_total(m)
        store(2 + m, done(m), (o_gate, o_up)[m])

    def ring_end_down():
        done(2)[...] = ring_total(2)
        back = remote(("back",), swap_out, swap_in, diagonal)
        sent.add(("back",))
        received.add(("back",))

        @pl.when(swapped)
        def _():
            swap_out[...] = done(2)[...].astype(BF)
            back.start()

        return back

    def down_done(back):
        @pl.when(swapped)
        def _():
            back.wait_recv()
            back.wait_send()
            done(2)[...] = swap_in[...].astype(F32)

        store(4, done(2), o_down)

    def ring(*steps):
        for m, s in steps:
            ring_send(m, s)

    w_start(0)
    w_start(1)
    swap_start()
    w_share(0)
    w_share(1)
    load_w[0].start()
    load_w[1].start()
    gate_col = slots()
    load_tok.wait()
    dispatch_t()
    self_par("t")
    self_nbr("t")
    y_own("t", 1, 3)
    load_cot.wait()
    dispatch_c(gate_col)
    t_own("t", 1)
    t_own("t", 3)
    y_oth("t", 1, 3, 2)
    t_nbr("t", 0)
    w_arrive(0, 1)
    w_arrive(1, 1)
    t_oth("t", 1)
    t_oth("t", 3)
    y_own("t", 2)
    w_arrive(0, 2)
    t_oth("t", 2)
    t_nbr("t", 1)
    w_arrive(1, 2)
    t_nbr("t", 3)
    t_own("t", 2)
    y_own("c", 1, 3)
    w_arrive(0, 3)
    self_nbr("c")
    t_nbr("t", 2)
    w_arrive(1, 3)
    swap_wait()
    w_start(2)
    w_share(2)
    y_oth("c", 1, 3, 2)
    self_par("c")
    w_arrive(0, 4)
    w_arrive(1, 4)
    t_own("c", 1)
    t_own("c", 3)
    t_oth("c", 1)
    t_oth("c", 3)
    y_own("c", 2)
    t_nbr("c", 0)
    gather_rows("t")
    w_arrive(2, 1)
    t_oth("c", 2)
    w_ready(0)
    w_ready(1)
    project_t()
    activate()
    t_own("c", 2)
    t_nbr("c", 1)
    t_nbr("c", 3)
    w_arrive(2, 2)
    t_nbr("c", 2)
    turn(x_t, x_buf, 0, nz)
    w_arrive(2, 3)
    turn(x_t, x_buf, nz, 2 * nz)
    w_arrive(2, 4)
    w_ready(2)
    gather_rows("c")
    project_c()
    drain("w", "ws")
    turn(g_t, g_buf, 0, nz)
    join_hidden()
    outputs()
    weight_grads("d", 1 - c, True)
    weight_grads("d", c, False)
    ring((2, 0))
    got("gh")
    feed(5)
    differentiate()
    weight_grads("gu", 1 - c, True)
    ring((2, 1))
    back_n("o", 2)
    back_n("o", 1)
    weight_grads("gu", c, False)
    ring((0, 0), (1, 0))
    feed(3)
    row_grads()
    feed(2)
    back_n("o", 3)
    back_n("o", 0)
    ring((2, 2))
    back_x("o", 2)
    back_x("o", 1)
    back_o("o", 2)
    back_o("o", 1)
    back_o("o", 3)
    back_x("o", 3)
    feed(1)
    back_o("o", 0)
    back_x("o", 0)
    ring((0, 1), (1, 1))
    back_n("g", 2)
    feed(1)
    back_n("g", 1)
    feed(1)
    back_x("g", 2)
    ring((2, 3))
    back_n("g", 3)
    feed(1)
    back_x("g", 1)
    ring((0, 2), (1, 2))
    back_n("g", 0)
    feed(1)
    back_x("g", 3)
    combine_o(gate_col)
    back_o("g", 2)
    feed(1)
    back_x("g", 0)
    swapping = ring_end_down()
    back_o("g", 1)
    ring((0, 3), (1, 3))
    back_o("g", 3)
    down_done(swapping)
    ring_end(0)
    ring_end(1)
    res_out(1)
    res_out(2)
    back_o("g", 0)
    res_out(0)
    res_out(3)
    drain()
    for copy in stored:
        copy.wait()


def finish(
    moe_in, res_in, sel_in, gate_in, up_in, down_in,
    moe_out, tok_out, gate_out, up_out, down_out,
    moe, res, sel, gate, up, down, tok, lsem, rsem, ssem,
):
    count = res.shape[-1] // BLK
    width = 2 * BLK
    loads, moves = [], []
    choose = pltpu.make_async_copy(sel_in, sel, lsem.at[4])
    choose.start()
    parts = []
    for j in range(count):
        at = pl.ds(j * BLK, BLK)
        parts.append(pltpu.make_async_copy(res_in.at[:, :, at], res.at[:, :, at], rsem.at[j]))
        parts[-1].start()
    whole = ((moe_in, moe, moe_out), (gate_in, gate, gate_out), (up_in, up, up_out), (down_in, down, down_out))
    for i, (a, v, b) in enumerate(whole):
        loads.append(pltpu.make_async_copy(a, v, lsem.at[i]))
        moves.append(pltpu.make_async_copy(v, b, ssem.at[i]))
        loads[-1].start()
    choose.wait()
    for j in range(count):
        parts[j].wait()
        rows_back = res[:, :, pl.ds(j * BLK, BLK)].reshape(8 * SLAB, BLK)
        for h in range(2):
            value = jnp.dot(sel[h], rows_back, preferred_element_type=F32)
            tok[:, pl.ds((2 * j + h) * BLK, BLK)] = value.astype(BF)
        at = pl.ds(j * width, width)
        moves.append(pltpu.make_async_copy(tok.at[:, at], tok_out.at[:, at], ssem.at[4 + j]))
        moves[-1].start()
        if j < 4:
            loads[j].wait()
            moves[j].start()
    for move in moves:
        move.wait()


def on_device(tokens, expert_ids, gate_values, cotangent, gate_weight, up_weight, down_weight):
    ntok, features = tokens.shape
    depth, units = gate_weight.shape
    nz = lax.axis_size("dp") // 2
    half = features // 2
    rows = 16 * CAP
    slab = (SLAB, half)
    small = (SLAB, half // 2)
    pair = (2,) + small
    shapes = (
        jax.ShapeDtypeStruct((ntok, features), BF),
        jax.ShapeDtypeStruct((ntok, features), BF),
        jax.ShapeDtypeStruct((depth, units), F32),
        jax.ShapeDtypeStruct((depth, units), F32),
        jax.ShapeDtypeStruct((depth, units), F32),
    )
    back = jax.ShapeDtypeStruct((8,) + slab, BF)
    chosen = jax.ShapeDtypeStruct((2, ntok, 8 * SLAB), BF)
    hbm, vmem = pl.BlockSpec(memory_space=pl.ANY), pl.BlockSpec(memory_space=pltpu.VMEM)
    results = pl.pallas_call(
        kernel,
        out_shape=(shapes[0], back, chosen) + shapes[2:],
        in_specs=[hbm, vmem, vmem, hbm, hbm, hbm, hbm],
        out_specs=(hbm,) * 6,
        scratch_shapes=[
            pltpu.VMEM((ntok, features), BF),
            pltpu.VMEM((ntok, features), BF),
            pltpu.VMEM((2, nz, depth, 3 * units), BF),
            pltpu.VMEM((2, nz, depth, 2 * units), BF),
            pltpu.VMEM((8,) + slab, BF),
            pltpu.VMEM((3,) + slab, BF),
            pltpu.VMEM((3,) + slab, BF),
            pltpu.VMEM((4,) + slab, BF),
            pltpu.VMEM((4,) + slab, BF),
            pltpu.VMEM((4,) + slab, BF),
            pltpu.VMEM((8,) + pair, BF),
            pltpu.VMEM((3,) + pair, BF),
            pltpu.VMEM((3,) + pair, BF),
            pltpu.VMEM((4,) + small, BF),
            pltpu.VMEM((4,) + pair, BF),
            pltpu.VMEM((4,) + small, BF),
            pltpu.VMEM((rows, features), BF),
            pltpu.VMEM((rows, half), BF),
            pltpu.VMEM((features, rows), BF),
            pltpu.VMEM((half, rows), BF),
            pltpu.VMEM((4,) + pair, BF),
            pltpu.VMEM((4,) + pair, BF),
            pltpu.VMEM((4,) + small, BF),
            pltpu.VMEM((4,) + small, BF),
            pltpu.VMEM((4,) + pair, BF),
            pltpu.VMEM((8,) + pair, BF),
            pltpu.VMEM((4, 4) + slab, BF),
            pltpu.VMEM((4,) + slab, BF),
            pltpu.VMEM((4,) + slab, BF),
            pltpu.VMEM((4,) + slab, BF),
            pltpu.VMEM((8,) + slab, BF),
            pltpu.VMEM((nz, depth, 3 * units), BF),
            pltpu.VMEM((21, depth, units), BF),
            pltpu.VMEM((rows, 4 * units), F32),
            pltpu.VMEM((rows, 2 * units), BF),
            pltpu.VMEM((2, rows, units), BF),
            pltpu.VMEM((rows, units), BF),
            pltpu.VMEM((rows, units), BF),
            pltpu.VMEM((rows, units), BF),
            pltpu.VMEM((depth, units), BF),
            pltpu.VMEM((depth, units), BF),
            pltpu.VMEM((2, ntok, 8 * SLAB), BF),
            pltpu.VMEM((2, 8 * SLAB, ntok), BF),
            pltpu.SemaphoreType.DMA((N_SEND,)),
            pltpu.SemaphoreType.DMA((N_RECV,)),
            pltpu.SemaphoreType.DMA((18,)),
        ],
        compiler_params=pltpu.CompilerParams(
            collective_id=0, has_side_effects=True, vmem_limit_bytes=62 * 1024 * 1024
        ),
        cost_estimate=pl.CostEstimate(
            flops=18 * rows * features * units, bytes_accessed=8 * ntok * features,
            transcendentals=2 * rows * units,
        ),
    )(
        tokens, expert_ids.reshape(1, ntok), gate_values.reshape(1, ntok), cotangent,
        gate_weight, up_weight, down_weight,
    )
    held = (shapes[0], back, chosen) + shapes[2:] + (shapes[1],)
    return pl.pallas_call(
        finish,
        out_shape=shapes,
        in_specs=[hbm] * 6,
        out_specs=(hbm,) * 5,
        scratch_shapes=[pltpu.VMEM(a.shape, a.dtype) for a in held]
        + [
            pltpu.SemaphoreType.DMA((5,)),
            pltpu.SemaphoreType.DMA((nz,)),
            pltpu.SemaphoreType.DMA((4 + nz,)),
        ],
        compiler_params=pltpu.CompilerParams(vmem_limit_bytes=62 * 1024 * 1024),
    )(*results)


def solution(mesh):
    rows, weights = P(("dp", "expert"), None), P("dp", "expert")
    return jax.shard_map(
        on_device,
        mesh=mesh,
        in_specs=(rows, rows, rows, rows, weights, weights, weights),
        out_specs=(rows, rows, weights, weights, weights),
        check_vma=False,
    )
```

```python
import math

import jax
import jax.numpy as jnp
from jax import lax
from jax.experimental import pallas as pl
from jax.experimental.pallas import tpu as pltpu
from jax.sharding import PartitionSpec as P

MESH = pl.DeviceIdType.MESH
BF, F32 = jnp.bfloat16, jnp.float32
HOPS = ({1: 4, -1: 3}, {1: 3, -1: 4}, {1: 4, -1: 3})
OWN, PAR, NBR, FWD = 0, 1, 2, 3
MIRROR = (PAR, OWN, FWD, NBR)
CAP = 24
SLAB = 2 * CAP
BLK = 256
PARTS = 4
N_SEND, N_RECV = 14, 123


def kernel(
    tok_hbm, ids, gv, cot_hbm, wg, wu, wd,
    o_moe, o_res, o_sel, o_gate, o_up, o_down,
    tok, cot, w_all, dw,
    s_t, own_t, oth_t, par_t, nbr_t, fwd_t, s_c, own_c, oth_c, par_c, nbr_c, fwd_c,
    x_buf, g_buf, x_t, g_t, out_own, out_nbr, out_par, out_fwd, out_oth, out_res,
    part, back_own, back_nbr, back_oth, res, sib_buf, ring_buf,
    pre, act, hid, hid_in, gh_out, gh_in, swap_out, swap_in, sel, sel_t, ssem, rsem, lsem,
):
    nz = w_all.shape[1]
    units = wg.shape[1]
    half = s_t.shape[-1]
    quarter = half // 2
    rows = x_buf.shape[0]
    group = rows // 4
    ntok = ids.shape[1]
    dp, ex = lax.axis_index("dp"), lax.axis_index("expert")
    z, c = lax.div(dp, 2), lax.rem(dp, 2)
    y, x = lax.div(ex, 4), lax.rem(ex, 4)
    p, hh = lax.div(x, 2), lax.rem(x, 2)
    partner = (dp, ex + 1 - 2 * hh)
    neighbour = (dp, y * 4 + 3 - x)
    sibling = (dp + 1 - 2 * c, ex)
    diagonal = (dp + 1 - 2 * c, ex + 1 - 2 * hh)
    swapped = c != hh

    def zpos(off):
        return lax.rem(z + nz + off, nz)

    def zdev(d):
        return (zpos(d) * 2 + c, ex)

    def ydev(r):
        return (dp, lax.rem(y + r, 4) * 4 + x)

    def expert_at(r, other):
        mine = lax.rem(y + r, 4) * 2 + p
        return mine + (1 - 2 * p) if other else mine

    def cols(m):
        return slice(m * units, (m + 1) * units)

    def block(j):
        return pl.ds(pl.multiple_of(j * BLK, BLK), BLK)

    shards = (wg, wu, wd)
    my_shard = [w_all.at[c, z, :, cols(m)] for m in range(3)]
    load_tok = pltpu.make_async_copy(tok_hbm, tok, lsem.at[0])
    load_cot = pltpu.make_async_copy(cot_hbm, cot, lsem.at[1])
    load_w = [pltpu.make_async_copy(shards[m], my_shard[m], lsem.at[2 + m]) for m in range(3)]
    load_tok.start()
    load_cot.start()

    barrier = pltpu.get_barrier_semaphore()
    for dev in (
        partner, neighbour, sibling, diagonal, zdev(1), zdev(-1), ydev(1), ydev(2), ydev(3)
    ):
        pl.semaphore_signal(barrier, inc=1, device_id=dev, device_id_type=MESH)
    copies, sizes, received, sent = {}, {}, set(), set()
    send_slots, recv_slots = {}, {}

    def send_group(key):
        if key[0] in ("own", "oth", "par", "nbr", "fwd"):
            return ("rows", key[1])
        if key[0] in ("bn", "bo", "bx", "ro", "rx"):
            return ("back", key[1])
        if key[0] in ("hid", "gh"):
            return ("units",)
        return key[:2] if key[0] in ("ws", "sib") else key[:1]

    def recv_group(key):
        if key[0] in ("par", "fwd"):
            return ("pair", key[1])
        return key[:2] if key[0] == "ws" else key

    def numbered(slots, name):
        return slots.setdefault(name, len(slots))

    def remote(key, src, dst, dev):
        i, j = numbered(send_slots, send_group(key)), numbered(recv_slots, recv_group(key))
        copies[key] = pltpu.make_async_remote_copy(
            src_ref=src, dst_ref=dst, send_sem=ssem.at[i], recv_sem=rsem.at[j],
            device_id=dev, device_id_type=MESH,
        )
        sizes[key] = src.shape
        return copies[key]

    def send(key, src, dst, dev):
        remote(key, src, dst, dev).start()

    piece_size = math.prod(ring_buf.shape[1:])

    def together(keys, i, j):
        total = sum(math.prod(sizes[k]) for k in keys)
        assert total % piece_size == 0
        ref = ring_buf.at[0:total // piece_size]
        return pltpu.make_async_remote_copy(
            src_ref=ref, dst_ref=ref, send_sem=ssem.at[i], recv_sem=rsem.at[j],
            device_id=partner, device_id_type=MESH,
        )

    def got(*key):
        name = recv_group(key)
        if name not in received:
            received.add(name)
            keys = [k for k in copies if recv_group(k) == name]
            if len(keys) == 1:
                copies[key].wait_recv()
            else:
                together(keys, 0, recv_slots[name]).wait_recv()

    def drain(*kinds):
        for name in send_slots:
            if name not in sent and (not kinds or name[0] in kinds):
                sent.add(name)
                keys = [k for k in copies if send_group(k) == name]
                together(keys, send_slots[name], 0).wait_send()

    def w_start(m):
        src = shards[m] if m < 2 else my_shard[m]
        for d in (1, -1):
            send(("w", m, d, 1), src, my_shard[m], zdev(d))

    def w_share(m):
        send(("ws", m, 0, 0), shards[m] if m < 2 else my_shard[m], my_shard[m], sibling)

    def w_arrive(m, s):
        for d in (1, -1):
            if s <= HOPS[m][d]:
                got("w", m, d, s)
                piece = w_all.at[c, zpos(-d * s), :, cols(m)]
                if s < HOPS[m][d]:
                    send(("w", m, d, s + 1), piece, piece, zdev(d))
                send(("ws", m, d, s), piece, piece, sibling)

    def w_ready(m):
        for d in (1, -1):
            for s in range(1, HOPS[m][d] + 1):
                got("w", m, d, s)
                got("ws", m, d, s)
        got("ws", m, 0, 0)
        if m < 2:
            load_w[m].wait()

    swap = remote(("swap",), wd, w_all.at[1 - c, z, :, cols(2)], diagonal)
    sent.add(("swap",))
    received.add(("swap",))

    def swap_start():
        @pl.when(swapped)
        def _():
            swap.start()

        @pl.when(jnp.logical_not(swapped))
        def _():
            load_w[2].start()

    def swap_wait():
        @pl.when(swapped)
        def _():
            swap.wait_recv()
            swap.wait_send()

        @pl.when(jnp.logical_not(swapped))
        def _():
            load_w[2].wait()

    stored = []

    def store(i, src, dst):
        stored.append(pltpu.make_async_copy(src, dst, lsem.at[5 + i]))
        stored[-1].start()

    def slots():
        lane = lax.broadcasted_iota(jnp.int32, (ntok, ntok), 1)
        down = lax.broadcasted_iota(jnp.int32, (ntok, ntok), 0)
        eye = down == lane
        idv = jnp.sum(
            jnp.where(eye, ids[...].astype(F32), 0.0), axis=1, keepdims=True
        ).astype(jnp.int32)
        gate = jnp.sum(jnp.where(eye, gv[...], 0.0), axis=1, keepdims=True)
        onehot = jnp.where(idv == lane, 1.0, 0.0).astype(F32)
        lower = jnp.where(down > lane, 1.0, 0.0).astype(BF)
        before = jnp.dot(lower, onehot.astype(BF), preferred_element_type=F32)
        order = jnp.sum(before * onehot, axis=1, keepdims=True).astype(jnp.int32)
        place = idv * SLAB + order
        slot = lax.broadcasted_iota(jnp.int32, (ntok, sel.shape[2]), 1)
        for k in range(2):
            chosen = jnp.where(slot == place + k * CAP, 1.0, 0.0)
            sel[k] = chosen.astype(BF)
            sel_t[k] = jnp.transpose(chosen).astype(BF)
        store(1, sel, o_sel)
        return gate

    by_cols = (((1,), (1,)), ((), ()))

    def spread(k, source, at):
        return jnp.dot(sel_t[k], source(at), preferred_element_type=F32)

    def dispatch_t():
        def body(j, carry):
            acc = spread(0, lambda at: tok[:, at], block(2 * j))
            acc = acc + spread(1, lambda at: tok[:, at], block(2 * j + 1))
            s_t[:, :, block(j)] = acc.astype(BF).reshape(8, SLAB, BLK)
            return carry

        lax.fori_loop(0, nz, body, 0)

    def dispatch_c(gate):
        def scaled(at):
            return (gate * cot[:, at].astype(F32)).astype(BF)

        def body(j, carry):
            for h in range(2):
                acc = spread(0, scaled, block(2 * j + h))
                acc = acc + spread(1, scaled, block(2 * (j + nz // 2) + h))
                s_c[:, h, :, block(j)] = acc.astype(BF).reshape(8, SLAB, BLK)
            return carry

        lax.fori_loop(0, nz // 2, body, 0)

    stores = {"t": (s_t, own_t, oth_t, par_t, nbr_t, fwd_t), "c": (s_c, own_c, oth_c, par_c, nbr_c, fwd_c)}

    def theirs(ph, ref):
        return ref if ph == "t" else ref.at[1 - hh]

    def y_own(ph, *hops):
        for r in hops:
            s, own = stores[ph][0], stores[ph][1]
            send(("own", ph, r), s.at[expert_at(r, False)], own.at[r - 1], ydev(r))

    def y_oth(ph, *hops):
        for r in hops:
            s, oth = stores[ph][0], stores[ph][2]
            send(("oth", ph, r), s.at[expert_at(r, True)], oth.at[r - 1], ydev(r))

    def self_par(ph):
        s, par = stores[ph][0], stores[ph][3]
        send(("par", ph, 0), theirs(ph, s.at[expert_at(0, False)]), par.at[0], partner)

    def self_nbr(ph):
        s, nbr = stores[ph][0], stores[ph][4]
        send(("nbr", ph, 0), s.at[expert_at(0, True)], nbr.at[0], neighbour)

    def t_own(ph, r):
        got("own", ph, r)
        own, par = stores[ph][1], stores[ph][3]
        send(("par", ph, r), theirs(ph, own.at[r - 1]), par.at[r], partner)

    def t_oth(ph, r):
        got("oth", ph, r)
        oth, nbr = stores[ph][2], stores[ph][4]
        send(("nbr", ph, r), oth.at[r - 1], nbr.at[r], neighbour)

    def t_nbr(ph, r):
        got("nbr", ph, r)
        nbr, fwd = stores[ph][4], stores[ph][5]
        send(("fwd", ph, r), theirs(ph, nbr.at[r]), fwd.at[r], partner)

    wide = 512

    def gather_rows(ph):
        s, own, oth, par, nbr, fwd = stores[ph]
        for r in range(4):
            got("par", ph, r)
            got("fwd", ph, r)

        def slab(g, r, at):
            if g == OWN:
                ref = s.at[expert_at(0, False)] if r == 0 else own.at[r - 1]
            else:
                ref = (None, par, nbr, fwd)[g].at[r]
            if ph == "c" and g in (OWN, NBR):
                ref = ref.at[hh]
            return ref[:, at].astype(F32)

        to_buf, width = (x_buf, half) if ph == "t" else (g_buf, quarter)

        def body(j, carry):
            at = pl.ds(pl.multiple_of(j * wide, wide), wide)
            for g in range(4):
                for r in (0, 2):
                    first, second = slab(g, r, at), slab(g, r + 1, at)
                    base = (g * 4 + r) * CAP
                    for h in range(2):
                        both = jnp.concatenate(
                            [first[h * CAP:(h + 1) * CAP], second[h * CAP:(h + 1) * CAP]], axis=0
                        )
                        to = pl.ds(pl.multiple_of(h * width + j * wide, wide), wide)
                        to_buf[base:base + SLAB, to] = both.astype(BF)
            return carry

        lax.fori_loop(0, width // wide, body, 0)

    def turn(to, source, start, stop):
        def body(j, carry):
            to[block(j), :] = jnp.transpose(source[:, block(j)])
            return carry

        lax.fori_loop(start, stop, body, 0)

    def project_t():
        to = slice(0, 2 * units)
        pre[:, to] = jnp.zeros((rows, 2 * units), F32)

        def body(j, carry):
            acc = None
            for k in range(2):
                term = jnp.dot(
                    x_buf[:, block(k * nz + j)], w_all[k, j, :, to], preferred_element_type=F32
                )
                acc = term if acc is None else acc + term
            pre[:, to] += acc
            return carry

        lax.fori_loop(0, nz, body, 0)

    def project_c():
        pre[:, 2 * units:] = jnp.zeros((rows, 2 * units), F32)

        def body(j, carry):
            for k in range(2):
                acc = None
                for i in range(2):
                    term = jnp.dot(
                        g_buf[:, block(2 * j + i)], w_all[k, 2 * j + i, :, cols(2)],
                        preferred_element_type=F32,
                    )
                    acc = term if acc is None else acc + term
                pre[:, cols(2 + k)] += acc
            return carry

        lax.fori_loop(0, nz // 2, body, 0)

        def pick(at, want):
            low = (want == 0).astype(F32)
            return pre[at, cols(2)] * low + pre[at, cols(3)] * (1.0 - low)

        def split(i, carry):
            at = pl.ds(pl.multiple_of(i * tall, tall), tall)
            gh_out[at, :] = pick(at, 1 - hh).astype(BF)
            pre[at, cols(2)] = pick(at, hh)
            return carry

        lax.fori_loop(0, rows // tall, split, 0)
        send(("gh",), gh_out, gh_in, partner)

    tall = 32

    def activate():
        def body(i, carry):
            at = pl.ds(pl.multiple_of(i * tall, tall), tall)
            gate, up = pre[at, cols(0)], pre[at, cols(1)]
            hid[hh, at, :] = (gate * jax.nn.sigmoid(gate) * up).astype(BF)
            return carry

        lax.fori_loop(0, rows // tall, body, 0)
        send(("hid",), hid.at[hh], hid_in, partner)

    def join_hidden():
        got("hid")
        for g in range(4):
            m = MIRROR[g]
            hid[1 - hh, g * group:(g + 1) * group, :] = hid_in[m * group:(m + 1) * group, :]

    def differentiate():
        got("gh")
        for g in range(4):
            def body(i, carry, g=g):
                at = pl.ds(pl.multiple_of(g * group + i * tall, tall), tall)
                there = pl.ds(pl.multiple_of(MIRROR[g] * group + i * tall, tall), tall)
                gate, up = pre[at, cols(0)], pre[at, cols(1)]
                grad = pre[at, cols(2)] + gh_in[there, :].astype(F32)
                sig = jax.nn.sigmoid(gate)
                act[at, cols(0)] = (grad * up * sig * (1.0 + gate * (1.0 - sig))).astype(BF)
                act[at, cols(1)] = (grad * (gate * sig)).astype(BF)
                return carry

            lax.fori_loop(0, group // tall, body, 0)

    def slabs(first, second):
        shape = (rows // CAP, CAP, BLK)
        joined = jnp.concatenate([first.reshape(shape), second.reshape(shape)], axis=1)
        return joined.astype(BF).reshape(4, 4, SLAB, BLK)

    def outputs():
        def body(j, carry):
            both = []
            for q in range(2):
                value = None
                for k in range(2):
                    term = lax.dot_general(
                        hid[k], w_all[k, j + q * (nz // 2), :, cols(2)], by_cols,
                        preferred_element_type=F32,
                    )
                    value = term if value is None else value + term
                both.append(value)
            joined = slabs(*both)
            out_own[:, hh, :, block(j)] = joined[OWN]
            out_nbr[:, hh, :, block(j)] = joined[NBR]
            out_par[:, :, block(j)] = joined[PAR]
            out_fwd[:, :, block(j)] = joined[FWD]
            return carry

        lax.fori_loop(0, nz // 2, body, 0)

    def row_grads():
        def body(j, carry):
            both = [
                lax.dot_general(
                    act[...], w_all[k, j, :, 0:2 * units], by_cols, preferred_element_type=F32
                )
                for k in range(2)
            ]
            part[:, :, :, block(j)] = slabs(*both)
            return carry

        lax.fori_loop(0, nz, body, 0)

    queue = []
    for turn_of in ("o", "g"):
        for kind in ("bn", "bo"):
            queue += [(kind, turn_of, r) for r in (2, 1, 3, 0)]

    def feed(count):
        for _ in range(count):
            kind, ph, r = queue.pop(0)
            if ph == "o":
                pairs = {"bn": (out_fwd.at[r], out_nbr.at[r, hh]), "bo": (out_par.at[r], out_own.at[r, hh])}
            else:
                pairs = {"bn": (part.at[FWD, r], back_nbr.at[r]), "bo": (part.at[PAR, r], back_own.at[r])}
            send((kind, ph, r), *pairs[kind], partner)

    def add_into(dst, a, b):
        def body(j, carry):
            at = pl.ds(pl.multiple_of(j * wide, wide), wide)
            dst[:, at] = (a[:, at].astype(F32) + b[:, at].astype(F32)).astype(BF)
            return carry

        lax.fori_loop(0, half // wide, body, 0)

    def back_n(ph, r):
        got("bn", ph, r)
        if ph == "o":
            mine, oth = out_nbr.at[r], out_oth
        else:
            mine, oth = part.at[NBR, r], back_oth
            add_into(mine, mine, back_nbr.at[r])
        send(("bx", ph, r), mine, oth.at[r], neighbour)

    def back_o(ph, r):
        got("bo", ph, r)
        e = expert_at(0, False)
        if ph == "o":
            mine, to = out_own.at[r], out_res.at[e]
            if r == 0:
                out_res[e] = out_own[0]
        else:
            mine, to = part.at[OWN, r], res.at[e]
            add_into(to if r == 0 else mine, mine, back_own.at[r])
        if r > 0:
            send(("ro", ph, r), mine, to, ydev(4 - r))

    def back_x(ph, r):
        got("bx", ph, r)
        e = expert_at(0, True)
        oth, to = (out_oth, out_res) if ph == "o" else (back_oth, res)
        if r == 0:
            to[e] = oth[0]
        else:
            send(("rx", ph, r), oth.at[r], to.at[e], ydev(4 - r))

    def combine_o(gate):
        for r in (1, 2, 3):
            got("ro", "o", r)
            got("rx", "o", r)

        def body(j, carry):
            for h in range(2):
                back = out_res[:, h, :, block(j)].reshape(8 * SLAB, BLK)
                for q in range(2):
                    value = gate * jnp.dot(sel[q], back, preferred_element_type=F32)
                    tok[:, block(2 * (j + q * (nz // 2)) + h)] = value.astype(BF)
            return carry

        lax.fori_loop(0, nz // 2, body, 0)
        store(0, tok, o_moe)

    def res_out(r):
        for i, other in enumerate((False, True)):
            if r > 0:
                got("rx" if other else "ro", "g", r)
            e = expert_at(r, other)
            store(5 + 2 * r + i, res.at[e], o_res.at[e])

    def grad_at(m, k, zz):
        ref = w_all if m == 2 else dw
        return ref.at[k, zz, :, cols(m)]

    ORDER = (4, 3, 5, 2, 6, 1, 7, 0)

    def offset(j):
        odd = lax.rem(j, 2)
        return 4 + lax.div(j, 2) * (1 - odd) - lax.div(j + 1, 2) * odd

    def weight_grads(kind, k, to_sibling):
        base = len(recv_slots)
        to, at_cols = (w_all, cols(2)) if kind == "d" else (dw, slice(0, 2 * units))
        if to_sibling:
            first = numbered(send_slots, ("sib", kind))

        def piece(j, off):
            return pltpu.make_async_remote_copy(
                src_ref=to.at[k, zpos(off), :, at_cols], dst_ref=sib_buf.at[off, :, at_cols],
                send_sem=ssem.at[first], recv_sem=rsem.at[base + j],
                device_id=sibling, device_id_type=MESH,
            )

        def body(j, carry):
            off = offset(j)
            zz = zpos(off)
            if kind == "d":
                value = jnp.dot(g_t[block(zz), :], hid[k], preferred_element_type=F32)
            else:
                value = jnp.dot(
                    x_t[block(k * nz + zz), :], act[...], preferred_element_type=F32
                )
            to[k, zz, :, at_cols] = value.astype(BF)
            if to_sibling:
                piece(j, off).start()
            return carry

        lax.fori_loop(0, nz, body, 0)
        if to_sibling:
            for j, off in enumerate(ORDER):
                key = ("sib", kind, off)
                numbered(recv_slots, key)
                copies[key] = piece(j, off)
                sizes[key] = (w_all.shape[2], units if kind == "d" else 2 * units)

    ring_slots = {}

    def slot_of(*key):
        return ring_buf.at[ring_slots.setdefault(key, len(ring_slots))]

    def local_sum(m, off):
        got("sib", "d" if m == 2 else "gu", off)
        mine = grad_at(m, c, zpos(off))
        return mine[...].astype(F32) + sib_buf[off, :, cols(m)].astype(F32)

    def ring_send(m, s):
        for d in (1, -1):
            hops = HOPS[m][d]
            if s < hops:
                off = (d * (hops - s)) % nz
                total = local_sum(m, off)
                if s > 0:
                    got("ring", m, d, s - 1)
                    total = total + slot_of(m, d, s - 1)[...].astype(F32)
                piece = grad_at(m, c, zpos(off))
                piece[...] = total.astype(BF)
                send(("ring", m, d, s), piece, slot_of(m, d, s), zdev(d))

    def ring_total(m):
        total = local_sum(m, 0)
        for d in (1, -1):
            last = HOPS[m][d] - 1
            got("ring", m, d, last)
            total = total + slot_of(m, d, last)[...].astype(F32)
        return total

    def done(m):
        return pre.at[0:w_all.shape[2], cols(m)]

    def ring_end(m):
        done(m)[...] = ring_total(m)
        store(2 + m, done(m), (o_gate, o_up)[m])

    def ring_end_down():
        done(2)[...] = ring_total(2)
        back = remote(("back",), swap_out, swap_in, diagonal)
        sent.add(("back",))
        received.add(("back",))

        @pl.when(swapped)
        def _():
            swap_out[...] = done(2)[...].astype(BF)
            back.start()

        return back

    def down_done(back):
        @pl.when(swapped)
        def _():
            back.wait_recv()
            back.wait_send()
            done(2)[...] = swap_in[...].astype(F32)

        store(4, done(2), o_down)

    def ring(*steps):
        for m, s in steps:
            ring_send(m, s)

    gate_col = slots()
    load_tok.wait()
    dispatch_t()
    pl.semaphore_wait(barrier, 9)
    w_start(0)
    w_start(1)
    self_par("t")
    self_nbr("t")
    y_own("t", 1, 3)
    swap_start()
    w_share(0)
    w_share(1)
    load_w[0].start()
    load_w[1].start()
    load_cot.wait()
    dispatch_c(gate_col)
    t_own("t", 1)
    t_own("t", 3)
    y_oth("t", 1, 3, 2)
    t_nbr("t", 0)
    w_arrive(0, 1)
    w_arrive(1, 1)
    swap_wait()
    w_start(2)
    w_share(2)
    t_oth("t", 1)
    t_oth("t", 3)
    y_own("t", 2)
    t_oth("t", 2)
    t_nbr("t", 1)
    t_nbr("t", 3)
    w_arrive(0, 2)
    w_arrive(1, 2)
    t_own("t", 2)
    w_arrive(2, 1)
    y_own("c", 1, 3)
    self_nbr("c")
    t_nbr("t", 2)
    y_oth("c", 1, 3, 2)
    self_par("c")
    t_own("c", 1)
    t_own("c", 3)
    t_oth("c", 1)
    t_oth("c", 3)
    y_own("c", 2)
    t_nbr("c", 0)
    w_arrive(0, 3)
    w_arrive(1, 3)
    w_arrive(2, 2)
    t_oth("c", 2)
    t_own("c", 2)
    t_nbr("c", 1)
    t_nbr("c", 3)
    gather_rows("t")
    w_arrive(0, 4)
    w_arrive(1, 4)
    w_arrive(2, 3)
    t_nbr("c", 2)
    w_ready(0)
    w_ready(1)
    project_t()
    activate()
    turn(x_t, x_buf, 0, 2 * nz)
    w_arrive(2, 4)
    w_ready(2)
    gather_rows("c")
    project_c()
    drain("w", "ws")
    turn(g_t, g_buf, 0, nz)
    join_hidden()
    outputs()
    weight_grads("d", 1 - c, True)
    weight_grads("d", c, False)
    ring((2, 0))
    got("gh")
    feed(5)
    differentiate()
    weight_grads("gu", 1 - c, True)
    ring((2, 1))
    back_n("o", 2)
    back_n("o", 1)
    weight_grads("gu", c, False)
    ring((0, 0), (1, 0))
    feed(3)
    row_grads()
    feed(2)
    back_n("o", 3)
    back_n("o", 0)
    ring((2, 2))
    back_x("o", 2)
    back_x("o", 1)
    back_o("o", 2)
    back_o("o", 1)
    back_o("o", 3)
    back_x("o", 3)
    feed(1)
    back_o("o", 0)
    back_x("o", 0)
    ring((0, 1), (1, 1))
    back_n("g", 2)
    feed(1)
    back_n("g", 1)
    feed(1)
    back_x("g", 2)
    ring((2, 3))
    back_n("g", 3)
    feed(1)
    back_x("g", 1)
    ring((0, 2), (1, 2))
    back_n("g", 0)
    feed(1)
    back_x("g", 3)
    combine_o(gate_col)
    back_o("g", 2)
    feed(1)
    back_x("g", 0)
    swapping = ring_end_down()
    back_o("g", 1)
    ring((0, 3), (1, 3))
    back_o("g", 3)
    down_done(swapping)
    ring_end(0)
    ring_end(1)
    res_out(1)
    res_out(2)
    back_o("g", 0)
    res_out(0)
    res_out(3)
    drain()
    for copy in stored:
        copy.wait()


def finish(
    moe_in, res_in, sel_in, gate_in, up_in, down_in,
    moe_out, tok_out, gate_out, up_out, down_out,
    moe, res, sel, gate, up, down, tok, lsem, rsem, ssem,
):
    count, wide = PARTS, res.shape[-1] // PARTS
    width = 2 * wide
    loads, moves = [], []
    choose = pltpu.make_async_copy(sel_in, sel, lsem.at[4])
    choose.start()
    parts = []
    for j in range(count):
        at = pl.ds(j * wide, wide)
        parts.append(pltpu.make_async_copy(res_in.at[:, :, at], res.at[:, :, at], rsem.at[j]))
        parts[-1].start()
    whole = ((moe_in, moe, moe_out), (gate_in, gate, gate_out), (up_in, up, up_out), (down_in, down, down_out))
    for i, (a, v, b) in enumerate(whole):
        loads.append(pltpu.make_async_copy(a, v, lsem.at[i]))
        moves.append(pltpu.make_async_copy(v, b, ssem.at[i]))
        loads[-1].start()
    choose.wait()
    for j in range(count):
        parts[j].wait()
        for i in range(j * wide // BLK, (j + 1) * wide // BLK):
            rows_back = res[:, :, pl.ds(i * BLK, BLK)].reshape(8 * SLAB, BLK)
            for h in range(2):
                value = jnp.dot(sel[h], rows_back, preferred_element_type=F32)
                tok[:, pl.ds((2 * i + h) * BLK, BLK)] = value.astype(BF)
        at = pl.ds(j * width, width)
        moves.append(pltpu.make_async_copy(tok.at[:, at], tok_out.at[:, at], ssem.at[4 + j]))
        moves[-1].start()
        for i in range(j * 4 // PARTS, (j + 1) * 4 // PARTS):
            loads[i].wait()
            moves[i].start()
    for move in moves:
        move.wait()


def on_device(tokens, expert_ids, gate_values, cotangent, gate_weight, up_weight, down_weight):
    ntok, features = tokens.shape
    depth, units = gate_weight.shape
    nz = lax.axis_size("dp") // 2
    half = features // 2
    rows = 16 * CAP
    slab = (SLAB, half)
    small = (SLAB, half // 2)
    pair = (2,) + small
    shapes = (
        jax.ShapeDtypeStruct((ntok, features), BF),
        jax.ShapeDtypeStruct((ntok, features), BF),
        jax.ShapeDtypeStruct((depth, units), F32),
        jax.ShapeDtypeStruct((depth, units), F32),
        jax.ShapeDtypeStruct((depth, units), F32),
    )
    back = jax.ShapeDtypeStruct((8,) + slab, BF)
    chosen = jax.ShapeDtypeStruct((2, ntok, 8 * SLAB), BF)
    hbm, vmem = pl.BlockSpec(memory_space=pl.ANY), pl.BlockSpec(memory_space=pltpu.VMEM)
    results = pl.pallas_call(
        kernel,
        out_shape=(shapes[0], back, chosen) + shapes[2:],
        in_specs=[hbm, vmem, vmem, hbm, hbm, hbm, hbm],
        out_specs=(hbm,) * 6,
        scratch_shapes=[
            pltpu.VMEM((ntok, features), BF),
            pltpu.VMEM((ntok, features), BF),
            pltpu.VMEM((2, nz, depth, 3 * units), BF),
            pltpu.VMEM((2, nz, depth, 2 * units), BF),
            pltpu.VMEM((8,) + slab, BF),
            pltpu.VMEM((3,) + slab, BF),
            pltpu.VMEM((3,) + slab, BF),
            pltpu.VMEM((4,) + slab, BF),
            pltpu.VMEM((4,) + slab, BF),
            pltpu.VMEM((4,) + slab, BF),
            pltpu.VMEM((8,) + pair, BF),
            pltpu.VMEM((3,) + pair, BF),
            pltpu.VMEM((3,) + pair, BF),
            pltpu.VMEM((4,) + small, BF),
            pltpu.VMEM((4,) + pair, BF),
            pltpu.VMEM((4,) + small, BF),
            pltpu.VMEM((rows, features), BF),
            pltpu.VMEM((rows, half), BF),
            pltpu.VMEM((features, rows), BF),
            pltpu.VMEM((half, rows), BF),
            pltpu.VMEM((4,) + pair, BF),
            pltpu.VMEM((4,) + pair, BF),
            pltpu.VMEM((4,) + small, BF),
            pltpu.VMEM((4,) + small, BF),
            pltpu.VMEM((4,) + pair, BF),
            pltpu.VMEM((8,) + pair, BF),
            pltpu.VMEM((4, 4) + slab, BF),
            pltpu.VMEM((4,) + slab, BF),
            pltpu.VMEM((4,) + slab, BF),
            pltpu.VMEM((4,) + slab, BF),
            pltpu.VMEM((8,) + slab, BF),
            pltpu.VMEM((nz, depth, 3 * units), BF),
            pltpu.VMEM((21, depth, units), BF),
            pltpu.VMEM((rows, 4 * units), F32),
            pltpu.VMEM((rows, 2 * units), BF),
            pltpu.VMEM((2, rows, units), BF),
            pltpu.VMEM((rows, units), BF),
            pltpu.VMEM((rows, units), BF),
            pltpu.VMEM((rows, units), BF),
            pltpu.VMEM((depth, units), BF),
            pltpu.VMEM((depth, units), BF),
            pltpu.VMEM((2, ntok, 8 * SLAB), BF),
            pltpu.VMEM((2, 8 * SLAB, ntok), BF),
            pltpu.SemaphoreType.DMA((N_SEND,)),
            pltpu.SemaphoreType.DMA((N_RECV,)),
            pltpu.SemaphoreType.DMA((18,)),
        ],
        compiler_params=pltpu.CompilerParams(
            collective_id=0, has_side_effects=True, vmem_limit_bytes=62 * 1024 * 1024
        ),
        cost_estimate=pl.CostEstimate(
            flops=18 * rows * features * units, bytes_accessed=8 * ntok * features,
            transcendentals=2 * rows * units,
        ),
    )(
        tokens, expert_ids.reshape(1, ntok), gate_values.reshape(1, ntok), cotangent,
        gate_weight, up_weight, down_weight,
    )
    held = (shapes[0], back, chosen) + shapes[2:] + (shapes[1],)
    return pl.pallas_call(
        finish,
        out_shape=shapes,
        in_specs=[hbm] * 6,
        out_specs=(hbm,) * 5,
        scratch_shapes=[pltpu.VMEM(a.shape, a.dtype) for a in held]
        + [
            pltpu.SemaphoreType.DMA((5,)),
            pltpu.SemaphoreType.DMA((nz,)),
            pltpu.SemaphoreType.DMA((4 + nz,)),
        ],
        compiler_params=pltpu.CompilerParams(vmem_limit_bytes=62 * 1024 * 1024),
    )(*results)


def solution(mesh):
    rows, weights = P(("dp", "expert"), None), P("dp", "expert")
    return jax.shard_map(
        on_device,
        mesh=mesh,
        in_specs=(rows, rows, rows, rows, weights, weights, weights),
        out_specs=(rows, rows, weights, weights, weights),
        check_vma=False,
    )
```

```python
import math

import jax
import jax.numpy as jnp
from jax import lax
from jax.experimental import pallas as pl
from jax.experimental.pallas import tpu as pltpu
from jax.sharding import PartitionSpec as P

MESH = pl.DeviceIdType.MESH
BF, F32 = jnp.bfloat16, jnp.float32
HOPS = ({1: 4, -1: 3}, {1: 3, -1: 4}, {1: 4, -1: 3})
OWN, PAR, NBR, FWD = 0, 1, 2, 3
MIRROR = (PAR, OWN, FWD, NBR)
CAP = 24
SLAB = 2 * CAP
BLK = 256
PARTS = 4
N_SEND, N_RECV = 14, 126


def kernel(
    tok_hbm, ids, gv, cot_hbm, wg, wu, wd,
    o_moe, o_res, o_sel, o_gate, o_up, o_down,
    tok, cot, w_all, dw,
    s_t, own_t, oth_t, par_t, nbr_t, fwd_t, s_c, own_c, oth_c, par_c, nbr_c, fwd_c,
    x_buf, g_buf, x_t, g_t, out_own, out_nbr, out_par, out_fwd, out_oth, out_res,
    part, back_own, back_nbr, back_oth, res, sib_buf, ring_buf,
    pre, act, hid, hid_in, gh_out, gh_in, swap_out, swap_in, sel, sel_t, ssem, rsem, lsem,
):
    nz = w_all.shape[1]
    units = wg.shape[1]
    half = s_t.shape[-1]
    quarter = half // 2
    rows = x_buf.shape[0]
    group = rows // 4
    ntok = ids.shape[1]
    dp, ex = lax.axis_index("dp"), lax.axis_index("expert")
    z, c = lax.div(dp, 2), lax.rem(dp, 2)
    y, x = lax.div(ex, 4), lax.rem(ex, 4)
    p, hh = lax.div(x, 2), lax.rem(x, 2)
    partner = (dp, ex + 1 - 2 * hh)
    neighbour = (dp, y * 4 + 3 - x)
    sibling = (dp + 1 - 2 * c, ex)
    diagonal = (dp + 1 - 2 * c, ex + 1 - 2 * hh)
    swapped = c != hh

    def zpos(off):
        return lax.rem(z + nz + off, nz)

    def zdev(d):
        return (zpos(d) * 2 + c, ex)

    def ydev(r):
        return (dp, lax.rem(y + r, 4) * 4 + x)

    def expert_at(r, other):
        mine = lax.rem(y + r, 4) * 2 + p
        return mine + (1 - 2 * p) if other else mine

    def cols(m):
        return slice(m * units, (m + 1) * units)

    def block(j):
        return pl.ds(pl.multiple_of(j * BLK, BLK), BLK)

    shards = (wg, wu, wd)
    my_shard = [w_all.at[c, z, :, cols(m)] for m in range(3)]
    load_tok = pltpu.make_async_copy(tok_hbm, tok, lsem.at[0])
    load_cot = pltpu.make_async_copy(cot_hbm, cot, lsem.at[1])
    load_w = [pltpu.make_async_copy(shards[m], my_shard[m], lsem.at[2 + m]) for m in range(3)]
    load_tok.start()
    load_cot.start()

    barrier = pltpu.get_barrier_semaphore()
    for dev in (
        partner, neighbour, sibling, diagonal, zdev(1), zdev(-1), ydev(1), ydev(2), ydev(3)
    ):
        pl.semaphore_signal(barrier, inc=1, device_id=dev, device_id_type=MESH)
    copies, sizes, received, sent = {}, {}, set(), set()
    send_slots, recv_slots = {}, {}

    def send_group(key):
        if key[0] in ("own", "oth", "par", "nbr", "fwd"):
            return ("rows", key[1])
        if key[0] in ("bn", "bo", "bx", "ro", "rx"):
            return ("back", key[1])
        if key[0] in ("hid", "gh"):
            return ("units",)
        return key[:2] if key[0] in ("ws", "sib") else key[:1]

    def recv_group(key):
        if key[0] in ("par", "fwd"):
            return key[:2]
        return key[:2] if key[0] == "ws" else key

    def numbered(slots, name):
        return slots.setdefault(name, len(slots))

    def remote(key, src, dst, dev):
        i, j = numbered(send_slots, send_group(key)), numbered(recv_slots, recv_group(key))
        copies[key] = pltpu.make_async_remote_copy(
            src_ref=src, dst_ref=dst, send_sem=ssem.at[i], recv_sem=rsem.at[j],
            device_id=dev, device_id_type=MESH,
        )
        sizes[key] = src.shape
        return copies[key]

    def send(key, src, dst, dev):
        remote(key, src, dst, dev).start()

    piece_size = math.prod(ring_buf.shape[1:])

    def together(keys, i, j):
        total = sum(math.prod(sizes[k]) for k in keys)
        assert total % piece_size == 0
        ref = ring_buf.at[0:total // piece_size]
        return pltpu.make_async_remote_copy(
            src_ref=ref, dst_ref=ref, send_sem=ssem.at[i], recv_sem=rsem.at[j],
            device_id=partner, device_id_type=MESH,
        )

    def got(*key):
        name = recv_group(key)
        if name not in received:
            received.add(name)
            keys = [k for k in copies if recv_group(k) == name]
            if len(keys) == 1:
                copies[key].wait_recv()
            else:
                together(keys, 0, recv_slots[name]).wait_recv()

    def drain(*kinds):
        for name in send_slots:
            if name not in sent and (not kinds or name[0] in kinds):
                sent.add(name)
                keys = [k for k in copies if send_group(k) == name]
                together(keys, send_slots[name], 0).wait_send()

    def w_start(m):
        src = shards[m] if m < 2 else my_shard[m]
        for d in (1, -1):
            send(("w", m, d, 1), src, my_shard[m], zdev(d))

    def w_share(m):
        send(("ws", m, 0, 0), shards[m] if m < 2 else my_shard[m], my_shard[m], sibling)

    def w_arrive(m, s):
        for d in (1, -1):
            if s <= HOPS[m][d]:
                got("w", m, d, s)
                piece = w_all.at[c, zpos(-d * s), :, cols(m)]
                if s < HOPS[m][d]:
                    send(("w", m, d, s + 1), piece, piece, zdev(d))
                send(("ws", m, d, s), piece, piece, sibling)

    def w_ready(m):
        for d in (1, -1):
            for s in range(1, HOPS[m][d] + 1):
                got("w", m, d, s)
                got("ws", m, d, s)
        got("ws", m, 0, 0)
        if m < 2:
            load_w[m].wait()

    swap = remote(("swap",), wd, w_all.at[1 - c, z, :, cols(2)], diagonal)
    sent.add(("swap",))
    received.add(("swap",))

    def swap_start():
        @pl.when(swapped)
        def _():
            swap.start()

        @pl.when(jnp.logical_not(swapped))
        def _():
            load_w[2].start()

    def swap_wait():
        @pl.when(swapped)
        def _():
            swap.wait_recv()
            swap.wait_send()

        @pl.when(jnp.logical_not(swapped))
        def _():
            load_w[2].wait()

    stored = []

    def store(i, src, dst):
        stored.append(pltpu.make_async_copy(src, dst, lsem.at[5 + i]))
        stored[-1].start()

    def slots():
        lane = lax.broadcasted_iota(jnp.int32, (ntok, ntok), 1)
        down = lax.broadcasted_iota(jnp.int32, (ntok, ntok), 0)
        eye = down == lane
        idv = jnp.sum(
            jnp.where(eye, ids[...].astype(F32), 0.0), axis=1, keepdims=True
        ).astype(jnp.int32)
        gate = jnp.sum(jnp.where(eye, gv[...], 0.0), axis=1, keepdims=True)
        onehot = jnp.where(idv == lane, 1.0, 0.0).astype(F32)
        lower = jnp.where(down > lane, 1.0, 0.0).astype(BF)
        before = jnp.dot(lower, onehot.astype(BF), preferred_element_type=F32)
        order = jnp.sum(before * onehot, axis=1, keepdims=True).astype(jnp.int32)
        place = idv * SLAB + order
        slot = lax.broadcasted_iota(jnp.int32, (ntok, sel.shape[2]), 1)
        for k in range(2):
            chosen = jnp.where(slot == place + k * CAP, 1.0, 0.0)
            sel[k] = chosen.astype(BF)
            sel_t[k] = jnp.transpose(chosen).astype(BF)
        store(1, sel, o_sel)
        return gate

    by_cols = (((1,), (1,)), ((), ()))

    def spread(k, source, at):
        return jnp.dot(sel_t[k], source(at), preferred_element_type=F32)

    def dispatch_t():
        def body(j, carry):
            acc = spread(0, lambda at: tok[:, at], block(2 * j))
            acc = acc + spread(1, lambda at: tok[:, at], block(2 * j + 1))
            s_t[:, :, block(j)] = acc.astype(BF).reshape(8, SLAB, BLK)
            return carry

        lax.fori_loop(0, nz, body, 0)

    def dispatch_c(gate):
        def scaled(at):
            return (gate * cot[:, at].astype(F32)).astype(BF)

        def body(j, carry):
            for h in range(2):
                acc = spread(0, scaled, block(2 * j + h))
                acc = acc + spread(1, scaled, block(2 * (j + nz // 2) + h))
                s_c[:, h, :, block(j)] = acc.astype(BF).reshape(8, SLAB, BLK)
            return carry

        lax.fori_loop(0, nz // 2, body, 0)

    stores = {"t": (s_t, own_t, oth_t, par_t, nbr_t, fwd_t), "c": (s_c, own_c, oth_c, par_c, nbr_c, fwd_c)}

    def theirs(ph, ref):
        return ref if ph == "t" else ref.at[1 - hh]

    def y_own(ph, *hops):
        for r in hops:
            s, own = stores[ph][0], stores[ph][1]
            send(("own", ph, r), s.at[expert_at(r, False)], own.at[r - 1], ydev(r))

    def y_oth(ph, *hops):
        for r in hops:
            s, oth = stores[ph][0], stores[ph][2]
            send(("oth", ph, r), s.at[expert_at(r, True)], oth.at[r - 1], ydev(r))

    def self_par(ph):
        s, par = stores[ph][0], stores[ph][3]
        send(("par", ph, 0), theirs(ph, s.at[expert_at(0, False)]), par.at[0], partner)

    def self_nbr(ph):
        s, nbr = stores[ph][0], stores[ph][4]
        send(("nbr", ph, 0), s.at[expert_at(0, True)], nbr.at[0], neighbour)

    def t_own(ph, r):
        got("own", ph, r)
        own, par = stores[ph][1], stores[ph][3]
        send(("par", ph, r), theirs(ph, own.at[r - 1]), par.at[r], partner)

    def t_oth(ph, r):
        got("oth", ph, r)
        oth, nbr = stores[ph][2], stores[ph][4]
        send(("nbr", ph, r), oth.at[r - 1], nbr.at[r], neighbour)

    def t_nbr(ph, r):
        got("nbr", ph, r)
        nbr, fwd = stores[ph][4], stores[ph][5]
        send(("fwd", ph, r), theirs(ph, nbr.at[r]), fwd.at[r], partner)

    wide = 512

    def gather_rows(ph, groups=(OWN, PAR, NBR, FWD)):
        s, own, oth, par, nbr, fwd = stores[ph]
        for r in range(4):
            if PAR in groups:
                got("par", ph, r)
            if FWD in groups:
                got("fwd", ph, r)

        def slab(g, r, at):
            if g == OWN:
                ref = s.at[expert_at(0, False)] if r == 0 else own.at[r - 1]
            else:
                ref = (None, par, nbr, fwd)[g].at[r]
            if ph == "c" and g in (OWN, NBR):
                ref = ref.at[hh]
            return ref[:, at].astype(F32)

        to_buf, width = (x_buf, half) if ph == "t" else (g_buf, quarter)

        def body(j, carry):
            at = pl.ds(pl.multiple_of(j * wide, wide), wide)
            for g in groups:
                for r in (0, 2):
                    first, second = slab(g, r, at), slab(g, r + 1, at)
                    base = (g * 4 + r) * CAP
                    for h in range(2):
                        both = jnp.concatenate(
                            [first[h * CAP:(h + 1) * CAP], second[h * CAP:(h + 1) * CAP]], axis=0
                        )
                        to = pl.ds(pl.multiple_of(h * width + j * wide, wide), wide)
                        to_buf[base:base + SLAB, to] = both.astype(BF)
            return carry

        lax.fori_loop(0, width // wide, body, 0)

    def turn(to, source, start, stop):
        def body(j, carry):
            to[block(j), :] = jnp.transpose(source[:, block(j)])
            return carry

        lax.fori_loop(start, stop, body, 0)

    def project_t():
        to = slice(0, 2 * units)
        pre[:, to] = jnp.zeros((rows, 2 * units), F32)

        def body(j, carry):
            acc = None
            for k in range(2):
                term = jnp.dot(
                    x_buf[:, block(k * nz + j)], w_all[k, j, :, to], preferred_element_type=F32
                )
                acc = term if acc is None else acc + term
            pre[:, to] += acc
            return carry

        lax.fori_loop(0, nz, body, 0)

    def project_c(part_of):
        count = rows // 2
        here = slice(part_of * count, (part_of + 1) * count)
        pre[here, 2 * units:] = jnp.zeros((count, 2 * units), F32)

        def body(j, carry):
            for k in range(2):
                acc = None
                for i in range(2):
                    term = jnp.dot(
                        g_buf[here, block(2 * j + i)], w_all[k, 2 * j + i, :, cols(2)],
                        preferred_element_type=F32,
                    )
                    acc = term if acc is None else acc + term
                pre[here, cols(2 + k)] += acc
            return carry

        lax.fori_loop(0, nz // 2, body, 0)

        def pick(at, want):
            low = (want == 0).astype(F32)
            return pre[at, cols(2)] * low + pre[at, cols(3)] * (1.0 - low)

        def split(i, carry):
            at = pl.ds(pl.multiple_of(part_of * count + i * tall, tall), tall)
            gh_out[at, :] = pick(at, 1 - hh).astype(BF)
            pre[at, cols(2)] = pick(at, hh)
            return carry

        lax.fori_loop(0, count // tall, split, 0)
        send(("gh", part_of), gh_out.at[here], gh_in.at[here], partner)

    tall = 32

    def activate():
        def body(i, carry):
            at = pl.ds(pl.multiple_of(i * tall, tall), tall)
            gate, up = pre[at, cols(0)], pre[at, cols(1)]
            hid[hh, at, :] = (gate * jax.nn.sigmoid(gate) * up).astype(BF)
            return carry

        lax.fori_loop(0, rows // tall, body, 0)
        send(("hid",), hid.at[hh], hid_in, partner)

    def join_hidden():
        got("hid")
        for g in range(4):
            m = MIRROR[g]
            hid[1 - hh, g * group:(g + 1) * group, :] = hid_in[m * group:(m + 1) * group, :]

    def differentiate():
        for g in range(4):
            got("gh", g // 2)

            def body(i, carry, g=g):
                at = pl.ds(pl.multiple_of(g * group + i * tall, tall), tall)
                there = pl.ds(pl.multiple_of(MIRROR[g] * group + i * tall, tall), tall)
                gate, up = pre[at, cols(0)], pre[at, cols(1)]
                grad = pre[at, cols(2)] + gh_in[there, :].astype(F32)
                sig = jax.nn.sigmoid(gate)
                act[at, cols(0)] = (grad * up * sig * (1.0 + gate * (1.0 - sig))).astype(BF)
                act[at, cols(1)] = (grad * (gate * sig)).astype(BF)
                return carry

            lax.fori_loop(0, group // tall, body, 0)

    def slabs(first, second):
        shape = (rows // CAP, CAP, BLK)
        joined = jnp.concatenate([first.reshape(shape), second.reshape(shape)], axis=1)
        return joined.astype(BF).reshape(4, 4, SLAB, BLK)

    def outputs():
        def body(j, carry):
            both = []
            for q in range(2):
                value = None
                for k in range(2):
                    term = lax.dot_general(
                        hid[k], w_all[k, j + q * (nz // 2), :, cols(2)], by_cols,
                        preferred_element_type=F32,
                    )
                    value = term if value is None else value + term
                both.append(value)
            joined = slabs(*both)
            out_own[:, hh, :, block(j)] = joined[OWN]
            out_nbr[:, hh, :, block(j)] = joined[NBR]
            out_par[:, :, block(j)] = joined[PAR]
            out_fwd[:, :, block(j)] = joined[FWD]
            return carry

        lax.fori_loop(0, nz // 2, body, 0)

    def row_grads():
        def body(j, carry):
            both = [
                lax.dot_general(
                    act[...], w_all[k, j, :, 0:2 * units], by_cols, preferred_element_type=F32
                )
                for k in range(2)
            ]
            part[:, :, :, block(j)] = slabs(*both)
            return carry

        lax.fori_loop(0, nz, body, 0)

    queue = []
    for turn_of in ("o", "g"):
        for kind in ("bn", "bo"):
            queue += [(kind, turn_of, r) for r in (2, 1, 3, 0)]

    def feed(count):
        for _ in range(count):
            kind, ph, r = queue.pop(0)
            if ph == "o":
                pairs = {"bn": (out_fwd.at[r], out_nbr.at[r, hh]), "bo": (out_par.at[r], out_own.at[r, hh])}
            else:
                pairs = {"bn": (part.at[FWD, r], back_nbr.at[r]), "bo": (part.at[PAR, r], back_own.at[r])}
            send((kind, ph, r), *pairs[kind], partner)

    def add_into(dst, a, b):
        def body(j, carry):
            at = pl.ds(pl.multiple_of(j * wide, wide), wide)
            dst[:, at] = (a[:, at].astype(F32) + b[:, at].astype(F32)).astype(BF)
            return carry

        lax.fori_loop(0, half // wide, body, 0)

    def back_n(ph, r):
        got("bn", ph, r)
        if ph == "o":
            mine, oth = out_nbr.at[r], out_oth
        else:
            mine, oth = part.at[NBR, r], back_oth
            add_into(mine, mine, back_nbr.at[r])
        send(("bx", ph, r), mine, oth.at[r], neighbour)

    def back_o(ph, r):
        got("bo", ph, r)
        e = expert_at(0, False)
        if ph == "o":
            mine, to = out_own.at[r], out_res.at[e]
            if r == 0:
                out_res[e] = out_own[0]
        else:
            mine, to = part.at[OWN, r], res.at[e]
            add_into(to if r == 0 else mine, mine, back_own.at[r])
        if r > 0:
            send(("ro", ph, r), mine, to, ydev(4 - r))

    def back_x(ph, r):
        got("bx", ph, r)
        e = expert_at(0, True)
        oth, to = (out_oth, out_res) if ph == "o" else (back_oth, res)
        if r == 0:
            to[e] = oth[0]
        else:
            send(("rx", ph, r), oth.at[r], to.at[e], ydev(4 - r))

    def combine_o(gate):
        for r in (1, 2, 3):
            got("ro", "o", r)
            got("rx", "o", r)

        def body(j, carry):
            for h in range(2):
                back = out_res[:, h, :, block(j)].reshape(8 * SLAB, BLK)
                for q in range(2):
                    value = gate * jnp.dot(sel[q], back, preferred_element_type=F32)
                    tok[:, block(2 * (j + q * (nz // 2)) + h)] = value.astype(BF)
            return carry

        lax.fori_loop(0, nz // 2, body, 0)
        store(0, tok, o_moe)

    def res_out(r):
        for i, other in enumerate((False, True)):
            if r > 0:
                got("rx" if other else "ro", "g", r)
            e = expert_at(r, other)
            store(5 + 2 * r + i, res.at[e], o_res.at[e])

    def grad_at(m, k, zz):
        ref = w_all if m == 2 else dw
        return ref.at[k, zz, :, cols(m)]

    ORDER = (4, 3, 5, 2, 6, 1, 7, 0)

    def offset(j):
        odd = lax.rem(j, 2)
        return 4 + lax.div(j, 2) * (1 - odd) - lax.div(j + 1, 2) * odd

    def weight_grads(kind, k, to_sibling):
        base = len(recv_slots)
        to, at_cols = (w_all, cols(2)) if kind == "d" else (dw, slice(0, 2 * units))
        if to_sibling:
            first = numbered(send_slots, ("sib", kind))

        def piece(j, off):
            return pltpu.make_async_remote_copy(
                src_ref=to.at[k, zpos(off), :, at_cols], dst_ref=sib_buf.at[off, :, at_cols],
                send_sem=ssem.at[first], recv_sem=rsem.at[base + j],
                device_id=sibling, device_id_type=MESH,
            )

        def body(j, carry):
            off = offset(j)
            zz = zpos(off)
            if kind == "d":
                value = jnp.dot(g_t[block(zz), :], hid[k], preferred_element_type=F32)
            else:
                value = jnp.dot(
                    x_t[block(k * nz + zz), :], act[...], preferred_element_type=F32
                )
            to[k, zz, :, at_cols] = value.astype(BF)
            if to_sibling:
                piece(j, off).start()
            return carry

        lax.fori_loop(0, nz, body, 0)
        if to_sibling:
            for j, off in enumerate(ORDER):
                key = ("sib", kind, off)
                numbered(recv_slots, key)
                copies[key] = piece(j, off)
                sizes[key] = (w_all.shape[2], units if kind == "d" else 2 * units)

    ring_slots = {}

    def slot_of(*key):
        return ring_buf.at[ring_slots.setdefault(key, len(ring_slots))]

    def local_sum(m, off):
        got("sib", "d" if m == 2 else "gu", off)
        mine = grad_at(m, c, zpos(off))
        return mine[...].astype(F32) + sib_buf[off, :, cols(m)].astype(F32)

    def ring_send(m, s):
        for d in (1, -1):
            hops = HOPS[m][d]
            if s < hops:
                off = (d * (hops - s)) % nz
                total = local_sum(m, off)
                if s > 0:
                    got("ring", m, d, s - 1)
                    total = total + slot_of(m, d, s - 1)[...].astype(F32)
                piece = grad_at(m, c, zpos(off))
                piece[...] = total.astype(BF)
                send(("ring", m, d, s), piece, slot_of(m, d, s), zdev(d))

    def ring_total(m):
        total = local_sum(m, 0)
        for d in (1, -1):
            last = HOPS[m][d] - 1
            got("ring", m, d, last)
            total = total + slot_of(m, d, last)[...].astype(F32)
        return total

    def done(m):
        return pre.at[0:w_all.shape[2], cols(m)]

    def ring_end(m):
        done(m)[...] = ring_total(m)
        store(2 + m, done(m), (o_gate, o_up)[m])

    def ring_end_down():
        done(2)[...] = ring_total(2)
        back = remote(("back",), swap_out, swap_in, diagonal)
        sent.add(("back",))
        received.add(("back",))

        @pl.when(swapped)
        def _():
            swap_out[...] = done(2)[...].astype(BF)
            back.start()

        return back

    def down_done(back):
        @pl.when(swapped)
        def _():
            back.wait_recv()
            back.wait_send()
            done(2)[...] = swap_in[...].astype(F32)

        store(4, done(2), o_down)

    def ring(*steps):
        for m, s in steps:
            ring_send(m, s)

    gate_col = slots()
    load_tok.wait()
    dispatch_t()
    pl.semaphore_wait(barrier, 9)
    w_start(0)
    w_start(1)
    self_par("t")
    self_nbr("t")
    y_own("t", 1, 3)
    swap_start()
    w_share(0)
    w_share(1)
    load_w[0].start()
    load_w[1].start()
    load_cot.wait()
    dispatch_c(gate_col)
    t_own("t", 1)
    t_own("t", 3)
    y_oth("t", 1, 3, 2)
    t_nbr("t", 0)
    w_arrive(0, 1)
    w_arrive(1, 1)
    swap_wait()
    w_start(2)
    w_share(2)
    t_oth("t", 1)
    t_oth("t", 3)
    y_own("t", 2)
    t_oth("t", 2)
    t_nbr("t", 1)
    t_nbr("t", 3)
    w_arrive(0, 2)
    w_arrive(1, 2)
    t_own("t", 2)
    w_arrive(2, 1)
    y_own("c", 1, 3)
    self_nbr("c")
    t_nbr("t", 2)
    y_oth("c", 1, 3, 2)
    self_par("c")
    t_own("c", 1)
    t_own("c", 3)
    t_oth("c", 1)
    t_oth("c", 3)
    y_own("c", 2)
    t_nbr("c", 0)
    w_arrive(0, 3)
    w_arrive(1, 3)
    w_arrive(2, 2)
    t_oth("c", 2)
    t_own("c", 2)
    t_nbr("c", 1)
    t_nbr("c", 3)
    gather_rows("t")
    w_arrive(0, 4)
    w_arrive(1, 4)
    w_arrive(2, 3)
    t_nbr("c", 2)
    w_ready(0)
    w_ready(1)
    project_t()
    activate()
    turn(x_t, x_buf, 0, 2 * nz)
    w_arrive(2, 4)
    w_ready(2)
    gather_rows("c", (OWN, PAR))
    project_c(0)
    gather_rows("c", (NBR, FWD))
    project_c(1)
    drain("w", "ws")
    turn(g_t, g_buf, 0, nz)
    join_hidden()
    outputs()
    weight_grads("d", 1 - c, True)
    weight_grads("d", c, False)
    ring((2, 0))
    got("gh", 0)
    got("gh", 1)
    feed(5)
    differentiate()
    weight_grads("gu", 1 - c, True)
    ring((2, 1))
    back_n("o", 2)
    back_n("o", 1)
    weight_grads("gu", c, False)
    ring((0, 0), (1, 0))
    feed(3)
    row_grads()
    feed(2)
    back_n("o", 3)
    back_n("o", 0)
    ring((2, 2))
    back_x("o", 2)
    back_x("o", 1)
    back_o("o", 2)
    back_o("o", 1)
    back_o("o", 3)
    back_x("o", 3)
    feed(1)
    back_o("o", 0)
    back_x("o", 0)
    ring((0, 1), (1, 1))
    back_n("g", 2)
    feed(1)
    back_n("g", 1)
    feed(1)
    back_x("g", 2)
    ring((2, 3))
    back_n("g", 3)
    feed(1)
    back_x("g", 1)
    ring((0, 2), (1, 2))
    back_n("g", 0)
    feed(1)
    back_x("g", 3)
    combine_o(gate_col)
    back_o("g", 2)
    feed(1)
    back_x("g", 0)
    swapping = ring_end_down()
    back_o("g", 1)
    ring((0, 3), (1, 3))
    back_o("g", 3)
    down_done(swapping)
    ring_end(0)
    ring_end(1)
    res_out(1)
    res_out(2)
    back_o("g", 0)
    res_out(0)
    res_out(3)
    drain()
    for copy in stored:
        copy.wait()


def finish(
    moe_in, res_in, sel_in, gate_in, up_in, down_in,
    moe_out, tok_out, gate_out, up_out, down_out,
    moe, res, sel, gate, up, down, tok, lsem, rsem, ssem,
):
    count, wide = PARTS, res.shape[-1] // PARTS
    width = 2 * wide
    loads, moves = [], []
    choose = pltpu.make_async_copy(sel_in, sel, lsem.at[4])
    choose.start()
    parts = []
    for j in range(count):
        at = pl.ds(j * wide, wide)
        parts.append(pltpu.make_async_copy(res_in.at[:, :, at], res.at[:, :, at], rsem.at[j]))
        parts[-1].start()
    whole = ((moe_in, moe, moe_out), (gate_in, gate, gate_out), (up_in, up, up_out), (down_in, down, down_out))
    for i, (a, v, b) in enumerate(whole):
        loads.append(pltpu.make_async_copy(a, v, lsem.at[i]))
        moves.append(pltpu.make_async_copy(v, b, ssem.at[i]))
        loads[-1].start()
    choose.wait()
    for j in range(count):
        parts[j].wait()
        for i in range(j * wide // BLK, (j + 1) * wide // BLK):
            rows_back = res[:, :, pl.ds(i * BLK, BLK)].reshape(8 * SLAB, BLK)
            for h in range(2):
                value = jnp.dot(sel[h], rows_back, preferred_element_type=F32)
                tok[:, pl.ds((2 * i + h) * BLK, BLK)] = value.astype(BF)
        at = pl.ds(j * width, width)
        moves.append(pltpu.make_async_copy(tok.at[:, at], tok_out.at[:, at], ssem.at[4 + j]))
        moves[-1].start()
        for i in range(j * 4 // PARTS, (j + 1) * 4 // PARTS):
            loads[i].wait()
            moves[i].start()
    for move in moves:
        move.wait()


def on_device(tokens, expert_ids, gate_values, cotangent, gate_weight, up_weight, down_weight):
    ntok, features = tokens.shape
    depth, units = gate_weight.shape
    nz = lax.axis_size("dp") // 2
    half = features // 2
    rows = 16 * CAP
    slab = (SLAB, half)
    small = (SLAB, half // 2)
    pair = (2,) + small
    shapes = (
        jax.ShapeDtypeStruct((ntok, features), BF),
        jax.ShapeDtypeStruct((ntok, features), BF),
        jax.ShapeDtypeStruct((depth, units), F32),
        jax.ShapeDtypeStruct((depth, units), F32),
        jax.ShapeDtypeStruct((depth, units), F32),
    )
    back = jax.ShapeDtypeStruct((8,) + slab, BF)
    chosen = jax.ShapeDtypeStruct((2, ntok, 8 * SLAB), BF)
    hbm, vmem = pl.BlockSpec(memory_space=pl.ANY), pl.BlockSpec(memory_space=pltpu.VMEM)
    results = pl.pallas_call(
        kernel,
        out_shape=(shapes[0], back, chosen) + shapes[2:],
        in_specs=[hbm, vmem, vmem, hbm, hbm, hbm, hbm],
        out_specs=(hbm,) * 6,
        scratch_shapes=[
            pltpu.VMEM((ntok, features), BF),
            pltpu.VMEM((ntok, features), BF),
            pltpu.VMEM((2, nz, depth, 3 * units), BF),
            pltpu.VMEM((2, nz, depth, 2 * units), BF),
            pltpu.VMEM((8,) + slab, BF),
            pltpu.VMEM((3,) + slab, BF),
            pltpu.VMEM((3,) + slab, BF),
            pltpu.VMEM((4,) + slab, BF),
            pltpu.VMEM((4,) + slab, BF),
            pltpu.VMEM((4,) + slab, BF),
            pltpu.VMEM((8,) + pair, BF),
            pltpu.VMEM((3,) + pair, BF),
            pltpu.VMEM((3,) + pair, BF),
            pltpu.VMEM((4,) + small, BF),
            pltpu.VMEM((4,) + pair, BF),
            pltpu.VMEM((4,) + small, BF),
            pltpu.VMEM((rows, features), BF),
            pltpu.VMEM((rows, half), BF),
            pltpu.VMEM((features, rows), BF),
            pltpu.VMEM((half, rows), BF),
            pltpu.VMEM((4,) + pair, BF),
            pltpu.VMEM((4,) + pair, BF),
            pltpu.VMEM((4,) + small, BF),
            pltpu.VMEM((4,) + small, BF),
            pltpu.VMEM((4,) + pair, BF),
            pltpu.VMEM((8,) + pair, BF),
            pltpu.VMEM((4, 4) + slab, BF),
            pltpu.VMEM((4,) + slab, BF),
            pltpu.VMEM((4,) + slab, BF),
            pltpu.VMEM((4,) + slab, BF),
            pltpu.VMEM((8,) + slab, BF),
            pltpu.VMEM((nz, depth, 3 * units), BF),
            pltpu.VMEM((21, depth, units), BF),
            pltpu.VMEM((rows, 4 * units), F32),
            pltpu.VMEM((rows, 2 * units), BF),
            pltpu.VMEM((2, rows, units), BF),
            pltpu.VMEM((rows, units), BF),
            pltpu.VMEM((rows, units), BF),
            pltpu.VMEM((rows, units), BF),
            pltpu.VMEM((depth, units), BF),
            pltpu.VMEM((depth, units), BF),
            pltpu.VMEM((2, ntok, 8 * SLAB), BF),
            pltpu.VMEM((2, 8 * SLAB, ntok), BF),
            pltpu.SemaphoreType.DMA((N_SEND,)),
            pltpu.SemaphoreType.DMA((N_RECV,)),
            pltpu.SemaphoreType.DMA((18,)),
        ],
        compiler_params=pltpu.CompilerParams(
            collective_id=0, has_side_effects=True, vmem_limit_bytes=62 * 1024 * 1024
        ),
        cost_estimate=pl.CostEstimate(
            flops=18 * rows * features * units, bytes_accessed=8 * ntok * features,
            transcendentals=2 * rows * units,
        ),
    )(
        tokens, expert_ids.reshape(1, ntok), gate_values.reshape(1, ntok), cotangent,
        gate_weight, up_weight, down_weight,
    )
    held = (shapes[0], back, chosen) + shapes[2:] + (shapes[1],)
    return pl.pallas_call(
        finish,
        out_shape=shapes,
        in_specs=[hbm] * 6,
        out_specs=(hbm,) * 5,
        scratch_shapes=[pltpu.VMEM(a.shape, a.dtype) for a in held]
        + [
            pltpu.SemaphoreType.DMA((5,)),
            pltpu.SemaphoreType.DMA((nz,)),
            pltpu.SemaphoreType.DMA((4 + nz,)),
        ],
        compiler_params=pltpu.CompilerParams(vmem_limit_bytes=62 * 1024 * 1024),
    )(*results)


def solution(mesh):
    rows, weights = P(("dp", "expert"), None), P("dp", "expert")
    return jax.shard_map(
        on_device,
        mesh=mesh,
        in_specs=(rows, rows, rows, rows, weights, weights, weights),
        out_specs=(rows, rows, weights, weights, weights),
        check_vma=False,
    )
```

```python
import math

import jax
import jax.numpy as jnp
from jax import lax
from jax.experimental import pallas as pl
from jax.experimental.pallas import tpu as pltpu
from jax.sharding import PartitionSpec as P

MESH = pl.DeviceIdType.MESH
BF, F32 = jnp.bfloat16, jnp.float32
HOPS = ({1: 4, -1: 3}, {1: 3, -1: 4}, {1: 4, -1: 3})
OWN, PAR, NBR, FWD = 0, 1, 2, 3
MIRROR = (PAR, OWN, FWD, NBR)
CAP = 24
SLAB = 2 * CAP
BLK = 256
PARTS = 4
N_SEND, N_RECV = 14, 126


def kernel(
    tok_hbm, ids, gv, cot_hbm, wg, wu, wd,
    o_moe, o_res, o_sel, o_gate, o_up, o_down,
    tok, cot, w_all, dw,
    s_t, own_t, oth_t, par_t, nbr_t, fwd_t, s_c, own_c, oth_c, par_c, nbr_c, fwd_c,
    x_buf, g_buf, x_t, g_t, out_own, out_nbr, out_par, out_fwd, out_oth, out_res,
    part, back_own, back_nbr, back_oth, res, sib_buf, ring_buf,
    pre, act, hid, hid_in, gh_out, gh_in, swap_out, swap_in, sel, sel_t, ssem, rsem, lsem,
):
    nz = w_all.shape[1]
    units = wg.shape[1]
    half = s_t.shape[-1]
    quarter = half // 2
    rows = x_buf.shape[0]
    group = rows // 4
    ntok = ids.shape[1]
    dp, ex = lax.axis_index("dp"), lax.axis_index("expert")
    z, c = lax.div(dp, 2), lax.rem(dp, 2)
    y, x = lax.div(ex, 4), lax.rem(ex, 4)
    p, hh = lax.div(x, 2), lax.rem(x, 2)
    partner = (dp, ex + 1 - 2 * hh)
    neighbour = (dp, y * 4 + 3 - x)
    sibling = (dp + 1 - 2 * c, ex)
    diagonal = (dp + 1 - 2 * c, ex + 1 - 2 * hh)
    swapped = c != hh

    def zpos(off):
        return lax.rem(z + nz + off, nz)

    def zdev(d):
        return (zpos(d) * 2 + c, ex)

    def ydev(r):
        return (dp, lax.rem(y + r, 4) * 4 + x)

    def expert_at(r, other):
        mine = lax.rem(y + r, 4) * 2 + p
        return mine + (1 - 2 * p) if other else mine

    def cols(m):
        return slice(m * units, (m + 1) * units)

    def block(j):
        return pl.ds(pl.multiple_of(j * BLK, BLK), BLK)

    shards = (wg, wu, wd)
    my_shard = [w_all.at[c, z, :, cols(m)] for m in range(3)]
    load_tok = pltpu.make_async_copy(tok_hbm, tok, lsem.at[0])
    load_cot = pltpu.make_async_copy(cot_hbm, cot, lsem.at[1])
    load_w = [pltpu.make_async_copy(shards[m], my_shard[m], lsem.at[2 + m]) for m in range(3)]
    load_tok.start()
    load_cot.start()

    barrier = pltpu.get_barrier_semaphore()
    for dev in (
        partner, neighbour, sibling, diagonal, zdev(1), zdev(-1), ydev(1), ydev(2), ydev(3)
    ):
        pl.semaphore_signal(barrier, inc=1, device_id=dev, device_id_type=MESH)
    copies, sizes, received, sent = {}, {}, set(), set()
    send_slots, recv_slots = {}, {}

    def send_group(key):
        if key[0] in ("own", "oth", "par", "nbr", "fwd"):
            return ("rows", key[1])
        if key[0] in ("bn", "bo", "bx", "ro", "rx"):
            return ("back", key[1])
        if key[0] in ("hid", "gh"):
            return ("units",)
        return key[:2] if key[0] in ("ws", "sib") else key[:1]

    def recv_group(key):
        if key[0] in ("par", "fwd"):
            return key[:2]
        return key[:2] if key[0] == "ws" else key

    def numbered(slots, name):
        return slots.setdefault(name, len(slots))

    def remote(key, src, dst, dev):
        i, j = numbered(send_slots, send_group(key)), numbered(recv_slots, recv_group(key))
        copies[key] = pltpu.make_async_remote_copy(
            src_ref=src, dst_ref=dst, send_sem=ssem.at[i], recv_sem=rsem.at[j],
            device_id=dev, device_id_type=MESH,
        )
        sizes[key] = src.shape
        return copies[key]

    def send(key, src, dst, dev):
        remote(key, src, dst, dev).start()

    piece_size = math.prod(ring_buf.shape[1:])

    def together(keys, i, j):
        total = sum(math.prod(sizes[k]) for k in keys)
        assert total % piece_size == 0
        ref = ring_buf.at[0:total // piece_size]
        return pltpu.make_async_remote_copy(
            src_ref=ref, dst_ref=ref, send_sem=ssem.at[i], recv_sem=rsem.at[j],
            device_id=partner, device_id_type=MESH,
        )

    def got(*key):
        name = recv_group(key)
        if name not in received:
            received.add(name)
            keys = [k for k in copies if recv_group(k) == name]
            if len(keys) == 1:
                copies[key].wait_recv()
            else:
                together(keys, 0, recv_slots[name]).wait_recv()

    def drain(*kinds):
        for name in send_slots:
            if name not in sent and (not kinds or name[0] in kinds):
                sent.add(name)
                keys = [k for k in copies if send_group(k) == name]
                together(keys, send_slots[name], 0).wait_send()

    def w_start(m):
        src = shards[m] if m < 2 else my_shard[m]
        for d in (1, -1):
            send(("w", m, d, 1), src, my_shard[m], zdev(d))

    def w_share(m):
        send(("ws", m, 0, 0), shards[m] if m < 2 else my_shard[m], my_shard[m], sibling)

    def w_arrive(m, s):
        for d in (1, -1):
            if s <= HOPS[m][d]:
                got("w", m, d, s)
                piece = w_all.at[c, zpos(-d * s), :, cols(m)]
                if s < HOPS[m][d]:
                    send(("w", m, d, s + 1), piece, piece, zdev(d))
                send(("ws", m, d, s), piece, piece, sibling)

    def w_ready(m):
        for d in (1, -1):
            for s in range(1, HOPS[m][d] + 1):
                got("w", m, d, s)
                got("ws", m, d, s)
        got("ws", m, 0, 0)
        if m < 2:
            load_w[m].wait()

    swap = remote(("swap",), wd, w_all.at[1 - c, z, :, cols(2)], diagonal)
    sent.add(("swap",))
    received.add(("swap",))

    def swap_start():
        @pl.when(swapped)
        def _():
            swap.start()

        @pl.when(jnp.logical_not(swapped))
        def _():
            load_w[2].start()

    def swap_wait():
        @pl.when(swapped)
        def _():
            swap.wait_recv()
            swap.wait_send()

        @pl.when(jnp.logical_not(swapped))
        def _():
            load_w[2].wait()

    stored = []

    def store(i, src, dst):
        stored.append(pltpu.make_async_copy(src, dst, lsem.at[5 + i]))
        stored[-1].start()

    def slots():
        lane = lax.broadcasted_iota(jnp.int32, (ntok, ntok), 1)
        down = lax.broadcasted_iota(jnp.int32, (ntok, ntok), 0)
        eye = down == lane
        idv = jnp.sum(
            jnp.where(eye, ids[...].astype(F32), 0.0), axis=1, keepdims=True
        ).astype(jnp.int32)
        gate = jnp.sum(jnp.where(eye, gv[...], 0.0), axis=1, keepdims=True)
        onehot = jnp.where(idv == lane, 1.0, 0.0).astype(F32)
        lower = jnp.where(down > lane, 1.0, 0.0).astype(BF)
        before = jnp.dot(lower, onehot.astype(BF), preferred_element_type=F32)
        order = jnp.sum(before * onehot, axis=1, keepdims=True).astype(jnp.int32)
        place = idv * SLAB + order
        slot = lax.broadcasted_iota(jnp.int32, (ntok, sel.shape[2]), 1)
        for k in range(2):
            chosen = jnp.where(slot == place + k * CAP, 1.0, 0.0)
            sel[k] = chosen.astype(BF)
            sel_t[k] = jnp.transpose(chosen).astype(BF)
        store(1, sel, o_sel)
        return gate

    by_cols = (((1,), (1,)), ((), ()))

    def spread(k, source, at):
        return jnp.dot(sel_t[k], source(at), preferred_element_type=F32)

    def dispatch_t():
        def body(j, carry):
            acc = spread(0, lambda at: tok[:, at], block(2 * j))
            acc = acc + spread(1, lambda at: tok[:, at], block(2 * j + 1))
            s_t[:, :, block(j)] = acc.astype(BF).reshape(8, SLAB, BLK)
            return carry

        lax.fori_loop(0, nz, body, 0)

    def dispatch_c(gate):
        def scaled(at):
            return (gate * cot[:, at].astype(F32)).astype(BF)

        def body(j, carry):
            for h in range(2):
                acc = spread(0, scaled, block(2 * j + h))
                acc = acc + spread(1, scaled, block(2 * (j + nz // 2) + h))
                s_c[:, h, :, block(j)] = acc.astype(BF).reshape(8, SLAB, BLK)
            return carry

        lax.fori_loop(0, nz // 2, body, 0)

    stores = {"t": (s_t, own_t, oth_t, par_t, nbr_t, fwd_t), "c": (s_c, own_c, oth_c, par_c, nbr_c, fwd_c)}

    def theirs(ph, ref):
        return ref if ph == "t" else ref.at[1 - hh]

    def y_own(ph, *hops):
        for r in hops:
            s, own = stores[ph][0], stores[ph][1]
            send(("own", ph, r), s.at[expert_at(r, False)], own.at[r - 1], ydev(r))

    def y_oth(ph, *hops):
        for r in hops:
            s, oth = stores[ph][0], stores[ph][2]
            send(("oth", ph, r), s.at[expert_at(r, True)], oth.at[r - 1], ydev(r))

    def self_par(ph):
        s, par = stores[ph][0], stores[ph][3]
        send(("par", ph, 0), theirs(ph, s.at[expert_at(0, False)]), par.at[0], partner)

    def self_nbr(ph):
        s, nbr = stores[ph][0], stores[ph][4]
        send(("nbr", ph, 0), s.at[expert_at(0, True)], nbr.at[0], neighbour)

    def t_own(ph, r):
        got("own", ph, r)
        own, par = stores[ph][1], stores[ph][3]
        send(("par", ph, r), theirs(ph, own.at[r - 1]), par.at[r], partner)

    def t_oth(ph, r):
        got("oth", ph, r)
        oth, nbr = stores[ph][2], stores[ph][4]
        send(("nbr", ph, r), oth.at[r - 1], nbr.at[r], neighbour)

    def t_nbr(ph, r):
        got("nbr", ph, r)
        nbr, fwd = stores[ph][4], stores[ph][5]
        send(("fwd", ph, r), theirs(ph, nbr.at[r]), fwd.at[r], partner)

    wide = 512

    def gather_rows(ph, groups=(OWN, PAR, NBR, FWD)):
        s, own, oth, par, nbr, fwd = stores[ph]
        for r in range(4):
            if PAR in groups:
                got("par", ph, r)
            if FWD in groups:
                got("fwd", ph, r)

        def slab(g, r, at):
            if g == OWN:
                ref = s.at[expert_at(0, False)] if r == 0 else own.at[r - 1]
            else:
                ref = (None, par, nbr, fwd)[g].at[r]
            if ph == "c" and g in (OWN, NBR):
                ref = ref.at[hh]
            return ref[:, at].astype(F32)

        to_buf, width = (x_buf, half) if ph == "t" else (g_buf, quarter)

        def body(j, carry):
            at = pl.ds(pl.multiple_of(j * wide, wide), wide)
            for g in groups:
                for r in (0, 2):
                    first, second = slab(g, r, at), slab(g, r + 1, at)
                    base = (g * 4 + r) * CAP
                    for h in range(2):
                        both = jnp.concatenate(
                            [first[h * CAP:(h + 1) * CAP], second[h * CAP:(h + 1) * CAP]], axis=0
                        )
                        to = pl.ds(pl.multiple_of(h * width + j * wide, wide), wide)
                        to_buf[base:base + SLAB, to] = both.astype(BF)
            return carry

        lax.fori_loop(0, width // wide, body, 0)

    def turn(to, source, start, stop):
        def body(j, carry):
            to[block(j), :] = jnp.transpose(source[:, block(j)])
            return carry

        lax.fori_loop(start, stop, body, 0)

    def project_t():
        to = slice(0, 2 * units)
        pre[:, to] = jnp.zeros((rows, 2 * units), F32)

        def body(j, carry):
            acc = None
            for k in range(2):
                term = jnp.dot(
                    x_buf[:, block(k * nz + j)], w_all[k, j, :, to], preferred_element_type=F32
                )
                acc = term if acc is None else acc + term
            pre[:, to] += acc
            return carry

        lax.fori_loop(0, nz, body, 0)

    def project_c(part_of):
        count = rows // 2
        here = slice(part_of * count, (part_of + 1) * count)
        pre[here, 2 * units:] = jnp.zeros((count, 2 * units), F32)

        def body(j, carry):
            for k in range(2):
                acc = None
                for i in range(2):
                    term = jnp.dot(
                        g_buf[here, block(2 * j + i)], w_all[k, 2 * j + i, :, cols(2)],
                        preferred_element_type=F32,
                    )
                    acc = term if acc is None else acc + term
                pre[here, cols(2 + k)] += acc
            return carry

        lax.fori_loop(0, nz // 2, body, 0)

        def pick(at, want):
            low = (want == 0).astype(F32)
            return pre[at, cols(2)] * low + pre[at, cols(3)] * (1.0 - low)

        def split(i, carry):
            at = pl.ds(pl.multiple_of(part_of * count + i * tall, tall), tall)
            gh_out[at, :] = pick(at, 1 - hh).astype(BF)
            pre[at, cols(2)] = pick(at, hh)
            return carry

        lax.fori_loop(0, count // tall, split, 0)
        send(("gh", part_of), gh_out.at[here], gh_in.at[here], partner)

    tall = 32

    def activate():
        def body(i, carry):
            at = pl.ds(pl.multiple_of(i * tall, tall), tall)
            gate, up = pre[at, cols(0)], pre[at, cols(1)]
            hid[hh, at, :] = (gate * jax.nn.sigmoid(gate) * up).astype(BF)
            return carry

        lax.fori_loop(0, rows // tall, body, 0)
        send(("hid",), hid.at[hh], hid_in, partner)

    def join_hidden():
        got("hid")
        for g in range(4):
            m = MIRROR[g]
            hid[1 - hh, g * group:(g + 1) * group, :] = hid_in[m * group:(m + 1) * group, :]

    def differentiate():
        for g in range(4):
            got("gh", g // 2)

            def body(i, carry, g=g):
                at = pl.ds(pl.multiple_of(g * group + i * tall, tall), tall)
                there = pl.ds(pl.multiple_of(MIRROR[g] * group + i * tall, tall), tall)
                gate, up = pre[at, cols(0)], pre[at, cols(1)]
                grad = pre[at, cols(2)] + gh_in[there, :].astype(F32)
                sig = jax.nn.sigmoid(gate)
                act[at, cols(0)] = (grad * up * sig * (1.0 + gate * (1.0 - sig))).astype(BF)
                act[at, cols(1)] = (grad * (gate * sig)).astype(BF)
                return carry

            lax.fori_loop(0, group // tall, body, 0)

    def slabs(first, second):
        shape = (rows // CAP, CAP, BLK)
        joined = jnp.concatenate([first.reshape(shape), second.reshape(shape)], axis=1)
        return joined.astype(BF).reshape(4, 4, SLAB, BLK)

    def outputs():
        def body(j, carry):
            both = []
            for q in range(2):
                value = None
                for k in range(2):
                    term = lax.dot_general(
                        hid[k], w_all[k, j + q * (nz // 2), :, cols(2)], by_cols,
                        preferred_element_type=F32,
                    )
                    value = term if value is None else value + term
                both.append(value)
            joined = slabs(*both)
            out_own[:, hh, :, block(j)] = joined[OWN]
            out_nbr[:, hh, :, block(j)] = joined[NBR]
            out_par[:, :, block(j)] = joined[PAR]
            out_fwd[:, :, block(j)] = joined[FWD]
            return carry

        lax.fori_loop(0, nz // 2, body, 0)

    def row_grads():
        def body(j, carry):
            both = [
                lax.dot_general(
                    act[...], w_all[k, j, :, 0:2 * units], by_cols, preferred_element_type=F32
                )
                for k in range(2)
            ]
            part[:, :, :, block(j)] = slabs(*both)
            return carry

        lax.fori_loop(0, nz, body, 0)

    queue = []
    for turn_of in ("o", "g"):
        for kind in ("bn", "bo"):
            queue += [(kind, turn_of, r) for r in (2, 1, 3, 0)]

    def feed(count):
        for _ in range(count):
            kind, ph, r = queue.pop(0)
            if ph == "o":
                pairs = {"bn": (out_fwd.at[r], out_nbr.at[r, hh]), "bo": (out_par.at[r], out_own.at[r, hh])}
            else:
                pairs = {"bn": (part.at[FWD, r], back_nbr.at[r]), "bo": (part.at[PAR, r], back_own.at[r])}
            send((kind, ph, r), *pairs[kind], partner)

    def add_into(dst, a, b):
        def body(j, carry):
            at = pl.ds(pl.multiple_of(j * wide, wide), wide)
            dst[:, at] = (a[:, at].astype(F32) + b[:, at].astype(F32)).astype(BF)
            return carry

        lax.fori_loop(0, half // wide, body, 0)

    def back_n(ph, r):
        got("bn", ph, r)
        if ph == "o":
            mine, oth = out_nbr.at[r], out_oth
        else:
            mine, oth = part.at[NBR, r], back_oth
            add_into(mine, mine, back_nbr.at[r])
        send(("bx", ph, r), mine, oth.at[r], neighbour)

    def back_o(ph, r):
        got("bo", ph, r)
        e = expert_at(0, False)
        if ph == "o":
            mine, to = out_own.at[r], out_res.at[e]
            if r == 0:
                out_res[e] = out_own[0]
        else:
            mine, to = part.at[OWN, r], res.at[e]
            add_into(to if r == 0 else mine, mine, back_own.at[r])
        if r > 0:
            send(("ro", ph, r), mine, to, ydev(4 - r))

    def back_x(ph, r):
        got("bx", ph, r)
        e = expert_at(0, True)
        oth, to = (out_oth, out_res) if ph == "o" else (back_oth, res)
        if r == 0:
            to[e] = oth[0]
        else:
            send(("rx", ph, r), oth.at[r], to.at[e], ydev(4 - r))

    def combine_o(gate):
        for r in (1, 2, 3):
            got("ro", "o", r)
            got("rx", "o", r)

        def body(j, carry):
            for h in range(2):
                back = out_res[:, h, :, block(j)].reshape(8 * SLAB, BLK)
                for q in range(2):
                    value = gate * jnp.dot(sel[q], back, preferred_element_type=F32)
                    tok[:, block(2 * (j + q * (nz // 2)) + h)] = value.astype(BF)
            return carry

        lax.fori_loop(0, nz // 2, body, 0)
        store(0, tok, o_moe)

    def res_out(r):
        for i, other in enumerate((False, True)):
            if r > 0:
                got("rx" if other else "ro", "g", r)
            e = expert_at(r, other)
            store(5 + 2 * r + i, res.at[e], o_res.at[e])

    def grad_at(m, k, zz):
        ref = w_all if m == 2 else dw
        return ref.at[k, zz, :, cols(m)]

    ORDER = (4, 3, 5, 2, 6, 1, 7, 0)

    def offset(j):
        odd = lax.rem(j, 2)
        return 4 + lax.div(j, 2) * (1 - odd) - lax.div(j + 1, 2) * odd

    def weight_grads(kind, k, to_sibling):
        base = len(recv_slots)
        to, at_cols = (w_all, cols(2)) if kind == "d" else (dw, slice(0, 2 * units))
        if to_sibling:
            first = numbered(send_slots, ("sib", kind))

        def piece(j, off):
            return pltpu.make_async_remote_copy(
                src_ref=to.at[k, zpos(off), :, at_cols], dst_ref=sib_buf.at[off, :, at_cols],
                send_sem=ssem.at[first], recv_sem=rsem.at[base + j],
                device_id=sibling, device_id_type=MESH,
            )

        def body(j, carry):
            off = offset(j)
            zz = zpos(off)
            if kind == "d":
                value = jnp.dot(g_t[block(zz), :], hid[k], preferred_element_type=F32)
            else:
                value = jnp.dot(
                    x_t[block(k * nz + zz), :], act[...], preferred_element_type=F32
                )
            to[k, zz, :, at_cols] = value.astype(BF)
            if to_sibling:
                piece(j, off).start()
            return carry

        lax.fori_loop(0, nz, body, 0)
        if to_sibling:
            for j, off in enumerate(ORDER):
                key = ("sib", kind, off)
                numbered(recv_slots, key)
                copies[key] = piece(j, off)
                sizes[key] = (w_all.shape[2], units if kind == "d" else 2 * units)

    ring_slots = {}

    def slot_of(*key):
        return ring_buf.at[ring_slots.setdefault(key, len(ring_slots))]

    def local_sum(m, off):
        got("sib", "d" if m == 2 else "gu", off)
        mine = grad_at(m, c, zpos(off))
        return mine[...].astype(F32) + sib_buf[off, :, cols(m)].astype(F32)

    def ring_send(m, s):
        for d in (1, -1):
            hops = HOPS[m][d]
            if s < hops:
                off = (d * (hops - s)) % nz
                total = local_sum(m, off)
                if s > 0:
                    got("ring", m, d, s - 1)
                    total = total + slot_of(m, d, s - 1)[...].astype(F32)
                piece = grad_at(m, c, zpos(off))
                piece[...] = total.astype(BF)
                send(("ring", m, d, s), piece, slot_of(m, d, s), zdev(d))

    def ring_total(m):
        total = local_sum(m, 0)
        for d in (1, -1):
            last = HOPS[m][d] - 1
            got("ring", m, d, last)
            total = total + slot_of(m, d, last)[...].astype(F32)
        return total

    def done(m):
        return pre.at[0:w_all.shape[2], cols(m)]

    def ring_end(m):
        done(m)[...] = ring_total(m)
        store(2 + m, done(m), (o_gate, o_up)[m])

    def ring_end_down():
        done(2)[...] = ring_total(2)
        back = remote(("back",), swap_out, swap_in, diagonal)
        sent.add(("back",))
        received.add(("back",))

        @pl.when(swapped)
        def _():
            swap_out[...] = done(2)[...].astype(BF)
            back.start()

        return back

    def down_done(back):
        @pl.when(swapped)
        def _():
            back.wait_recv()
            back.wait_send()
            done(2)[...] = swap_in[...].astype(F32)

        store(4, done(2), o_down)

    def ring(*steps):
        for m, s in steps:
            ring_send(m, s)

    gate_col = slots()
    load_tok.wait()
    dispatch_t()
    pl.semaphore_wait(barrier, 9)
    w_start(0)
    w_start(1)
    self_par("t")
    self_nbr("t")
    y_own("t", 1, 3)
    swap_start()
    w_share(0)
    w_share(1)
    load_w[0].start()
    load_w[1].start()
    load_cot.wait()
    dispatch_c(gate_col)
    t_own("t", 1)
    t_own("t", 3)
    y_oth("t", 1, 3, 2)
    t_nbr("t", 0)
    w_arrive(0, 1)
    w_arrive(1, 1)
    swap_wait()
    w_start(2)
    w_share(2)
    t_oth("t", 1)
    t_oth("t", 3)
    y_own("t", 2)
    t_oth("t", 2)
    t_nbr("t", 1)
    t_nbr("t", 3)
    w_arrive(0, 2)
    w_arrive(1, 2)
    t_own("t", 2)
    w_arrive(2, 1)
    y_own("c", 1, 3)
    self_nbr("c")
    t_nbr("t", 2)
    y_oth("c", 1, 3, 2)
    self_par("c")
    t_own("c", 1)
    t_own("c", 3)
    t_oth("c", 1)
    t_oth("c", 3)
    y_own("c", 2)
    t_nbr("c", 0)
    w_arrive(0, 3)
    w_arrive(1, 3)
    w_arrive(2, 2)
    t_oth("c", 2)
    t_own("c", 2)
    t_nbr("c", 1)
    t_nbr("c", 3)
    gather_rows("t")
    w_arrive(0, 4)
    w_arrive(1, 4)
    w_arrive(2, 3)
    t_nbr("c", 2)
    w_ready(0)
    w_ready(1)
    project_t()
    activate()
    turn(x_t, x_buf, 0, 2 * nz)
    w_arrive(2, 4)
    w_ready(2)
    gather_rows("c", (OWN, PAR))
    project_c(0)
    gather_rows("c", (NBR, FWD))
    project_c(1)
    drain("w", "ws")
    turn(g_t, g_buf, 0, nz)
    join_hidden()
    outputs()
    weight_grads("d", 1 - c, True)
    weight_grads("d", c, False)
    ring((2, 0))
    got("gh", 0)
    got("gh", 1)
    feed(5)
    differentiate()
    weight_grads("gu", 1 - c, True)
    ring((2, 1))
    back_n("o", 2)
    back_n("o", 1)
    weight_grads("gu", c, False)
    ring((0, 0), (1, 0))
    feed(3)
    row_grads()
    feed(2)
    back_n("o", 3)
    back_n("o", 0)
    ring((2, 2))
    back_x("o", 2)
    back_x("o", 1)
    back_o("o", 2)
    back_o("o", 1)
    back_o("o", 3)
    back_x("o", 3)
    feed(1)
    back_o("o", 0)
    back_x("o", 0)
    ring((0, 1), (1, 1))
    back_n("g", 2)
    feed(1)
    back_n("g", 1)
    feed(1)
    back_x("g", 2)
    ring((2, 3))
    back_n("g", 3)
    feed(1)
    back_x("g", 1)
    ring((0, 2), (1, 2))
    back_n("g", 0)
    feed(1)
    back_x("g", 3)
    combine_o(gate_col)
    back_o("g", 2)
    feed(1)
    back_x("g", 0)
    swapping = ring_end_down()
    back_o("g", 1)
    ring((0, 3), (1, 3))
    back_o("g", 3)
    down_done(swapping)
    ring_end(0)
    ring_end(1)
    res_out(1)
    res_out(2)
    back_o("g", 0)
    res_out(0)
    res_out(3)
    drain()
    for copy in stored:
        copy.wait()


def finish(
    moe_in, res_in, sel_in, gate_in, up_in, down_in,
    moe_out, tok_out, gate_out, up_out, down_out,
    moe, res, sel, gate, up, down, tok, lsem, rsem, ssem,
):
    count, wide = PARTS, res.shape[-1] // PARTS
    width = 2 * wide
    loads, moves = [], []
    choose = pltpu.make_async_copy(sel_in, sel, lsem.at[4])
    choose.start()
    parts = []
    for j in range(count):
        at = pl.ds(j * wide, wide)
        parts.append(pltpu.make_async_copy(res_in.at[:, :, at], res.at[:, :, at], rsem.at[j]))
        parts[-1].start()
    whole = ((moe_in, moe, moe_out), (gate_in, gate, gate_out), (up_in, up, up_out), (down_in, down, down_out))
    for i, (a, v, b) in enumerate(whole):
        loads.append(pltpu.make_async_copy(a, v, lsem.at[i]))
        moves.append(pltpu.make_async_copy(v, b, ssem.at[i]))
        loads[-1].start()
    choose.wait()
    for j in range(count):
        parts[j].wait()
        for i in range(j * 4 // PARTS, (j + 1) * 4 // PARTS):
            loads[i].wait()
            moves[i].start()
        for i in range(j * wide // BLK, (j + 1) * wide // BLK):
            rows_back = res[:, :, pl.ds(i * BLK, BLK)].reshape(8 * SLAB, BLK)
            for h in range(2):
                value = jnp.dot(sel[h], rows_back, preferred_element_type=F32)
                tok[:, pl.ds((2 * i + h) * BLK, BLK)] = value.astype(BF)
        at = pl.ds(j * width, width)
        moves.append(pltpu.make_async_copy(tok.at[:, at], tok_out.at[:, at], ssem.at[4 + j]))
        moves[-1].start()
    for move in moves:
        move.wait()


def on_device(tokens, expert_ids, gate_values, cotangent, gate_weight, up_weight, down_weight):
    ntok, features = tokens.shape
    depth, units = gate_weight.shape
    nz = lax.axis_size("dp") // 2
    half = features // 2
    rows = 16 * CAP
    slab = (SLAB, half)
    small = (SLAB, half // 2)
    pair = (2,) + small
    shapes = (
        jax.ShapeDtypeStruct((ntok, features), BF),
        jax.ShapeDtypeStruct((ntok, features), BF),
        jax.ShapeDtypeStruct((depth, units), F32),
        jax.ShapeDtypeStruct((depth, units), F32),
        jax.ShapeDtypeStruct((depth, units), F32),
    )
    back = jax.ShapeDtypeStruct((8,) + slab, BF)
    chosen = jax.ShapeDtypeStruct((2, ntok, 8 * SLAB), BF)
    hbm, vmem = pl.BlockSpec(memory_space=pl.ANY), pl.BlockSpec(memory_space=pltpu.VMEM)
    results = pl.pallas_call(
        kernel,
        out_shape=(shapes[0], back, chosen) + shapes[2:],
        in_specs=[hbm, vmem, vmem, hbm, hbm, hbm, hbm],
        out_specs=(hbm,) * 6,
        scratch_shapes=[
            pltpu.VMEM((ntok, features), BF),
            pltpu.VMEM((ntok, features), BF),
            pltpu.VMEM((2, nz, depth, 3 * units), BF),
            pltpu.VMEM((2, nz, depth, 2 * units), BF),
            pltpu.VMEM((8,) + slab, BF),
            pltpu.VMEM((3,) + slab, BF),
            pltpu.VMEM((3,) + slab, BF),
            pltpu.VMEM((4,) + slab, BF),
            pltpu.VMEM((4,) + slab, BF),
            pltpu.VMEM((4,) + slab, BF),
            pltpu.VMEM((8,) + pair, BF),
            pltpu.VMEM((3,) + pair, BF),
            pltpu.VMEM((3,) + pair, BF),
            pltpu.VMEM((4,) + small, BF),
            pltpu.VMEM((4,) + pair, BF),
            pltpu.VMEM((4,) + small, BF),
            pltpu.VMEM((rows, features), BF),
            pltpu.VMEM((rows, half), BF),
            pltpu.VMEM((features, rows), BF),
            pltpu.VMEM((half, rows), BF),
            pltpu.VMEM((4,) + pair, BF),
            pltpu.VMEM((4,) + pair, BF),
            pltpu.VMEM((4,) + small, BF),
            pltpu.VMEM((4,) + small, BF),
            pltpu.VMEM((4,) + pair, BF),
            pltpu.VMEM((8,) + pair, BF),
            pltpu.VMEM((4, 4) + slab, BF),
            pltpu.VMEM((4,) + slab, BF),
            pltpu.VMEM((4,) + slab, BF),
            pltpu.VMEM((4,) + slab, BF),
            pltpu.VMEM((8,) + slab, BF),
            pltpu.VMEM((nz, depth, 3 * units), BF),
            pltpu.VMEM((21, depth, units), BF),
            pltpu.VMEM((rows, 4 * units), F32),
            pltpu.VMEM((rows, 2 * units), BF),
            pltpu.VMEM((2, rows, units), BF),
            pltpu.VMEM((rows, units), BF),
            pltpu.VMEM((rows, units), BF),
            pltpu.VMEM((rows, units), BF),
            pltpu.VMEM((depth, units), BF),
            pltpu.VMEM((depth, units), BF),
            pltpu.VMEM((2, ntok, 8 * SLAB), BF),
            pltpu.VMEM((2, 8 * SLAB, ntok), BF),
            pltpu.SemaphoreType.DMA((N_SEND,)),
            pltpu.SemaphoreType.DMA((N_RECV,)),
            pltpu.SemaphoreType.DMA((18,)),
        ],
        compiler_params=pltpu.CompilerParams(
            collective_id=0, has_side_effects=True, vmem_limit_bytes=62 * 1024 * 1024
        ),
        cost_estimate=pl.CostEstimate(
            flops=18 * rows * features * units, bytes_accessed=8 * ntok * features,
            transcendentals=2 * rows * units,
        ),
    )(
        tokens, expert_ids.reshape(1, ntok), gate_values.reshape(1, ntok), cotangent,
        gate_weight, up_weight, down_weight,
    )
    held = (shapes[0], back, chosen) + shapes[2:] + (shapes[1],)
    return pl.pallas_call(
        finish,
        out_shape=shapes,
        in_specs=[hbm] * 6,
        out_specs=(hbm,) * 5,
        scratch_shapes=[pltpu.VMEM(a.shape, a.dtype) for a in held]
        + [
            pltpu.SemaphoreType.DMA((5,)),
            pltpu.SemaphoreType.DMA((nz,)),
            pltpu.SemaphoreType.DMA((4 + nz,)),
        ],
        compiler_params=pltpu.CompilerParams(vmem_limit_bytes=62 * 1024 * 1024),
    )(*results)


def solution(mesh):
    rows, weights = P(("dp", "expert"), None), P("dp", "expert")
    return jax.shard_map(
        on_device,
        mesh=mesh,
        in_specs=(rows, rows, rows, rows, weights, weights, weights),
        out_specs=(rows, rows, weights, weights, weights),
        check_vma=False,
    )
```
